512 devices in a mesh: sector: 64 (over x, z), term: 8 (over y, core).
Axes of the slice: x: 4, y: 4, z: 16, core: 2. Of those that a mesh axis runs over, the one named last changes fastest.
Arguments:
- wavefunction: bfloat16 [8192, 8192], P('sector'), may hold values from -6 to 6
- left_env: bfloat16 [8, 64, 128, 128], P('term', 'sector'), may hold values from -0.1875 to 0.1875
- right_env: bfloat16 [8, 64, 128, 128], P('term', 'sector'), may hold values from -0.5 to 0.5
- left_sizes: int32 [64], replicated, may hold values from 1 to 128, 6144 in all
- right_sizes: int32 [64], replicated, may hold values from 1 to 128, 6144 in all
- charge_left: int32 [64], replicated, may hold values from 0 to 3
- charge_right: int32 [64], replicated, may hold values from 0 to 3
- term_shift: int32 [8], P('term'), may hold values from -1 to 1
Outputs:
- product: bfloat16 [8192, 8192], P('sector', 'term')
The draws below stay inside these ranges and needn't reach their ends.
Inputs may be any that keep to these rules, and one draw needn't show every extreme that they name: `left_sizes`: some left block holds all 128 states; the sizes sum to 6144. `right_sizes`: some right block holds all 128 states; the sizes sum to 6144.
All inputs are finite; a program needn't handle non-finite values.
Results may differ from the reference program's by a relative error of at most 0.019.
Values may be sent and summed in bfloat16 or wider, within the bound.
A program may use at most 64 MiB of HBM per device.

```python
import math
import jax
import jax.numpy as jnp
import numpy as np
from jax import lax

CAP = 128
SECTORS = 64
BOND = 8192
TERMS = 8


def set_ends(entries, own_key, least, largest):
    shape = entries.shape
    spot = [jax.random.randint(jax.random.fold_in(own_key, axis), (), 0, shape[axis]) for axis in range(len(shape))]
    entries = entries.at[tuple(spot)].set(least)
    longest = shape.index(max(shape))
    spot[longest] = (spot[longest] + 1) % shape[longest]
    return entries.at[tuple(spot)].set(largest)


def block_scale(stream_key, shape, pieces, low, top_value):
    def one(position, parts):
        heights = jax.random.uniform(jax.random.fold_in(jax.random.fold_in(stream_key, 6), position), (parts,), jnp.float32, low / len(pieces), top_value / len(pieces))
        return jnp.repeat(jnp.exp(heights), shape[position] // parts).reshape((-1,) + (1,) * (len(shape) - position - 1))

    factor_of = one(*pieces[0])
    for cut in pieces[1:]:
        factor_of = factor_of * one(*cut)
    return factor_of


def split_up(number_of, total, most, skew):
    loads = [(1 << 20) // math.isqrt(standing ** skew) + 1 for standing in range(2, number_of + 1)]
    rest, holding = total - most - (number_of - 1), [1] * (number_of - 1)
    while rest > 0:
        candidates = [i for i in range(number_of - 1) if holding[i] < most]
        pool, budget = sum([loads[i] for i in candidates]), rest
        for i in candidates:
            extra = min(most - holding[i], max(1, budget * loads[i] // pool), rest)
            holding[i] = holding[i] + extra
            rest = rest - extra
    return np.array([most] + holding)


def ragged(own_key, amount, total, reach, lean):
    if amount == 2:
        one = jax.random.randint(own_key, (), max(1, total - reach), min(reach, total - 1) + 1)
        return jnp.stack([one, total - one])
    tallies = jnp.asarray(split_up(amount, total, reach, lean), jnp.int32)
    twos = (amount - 1) // 2
    donor, receiver = tallies[1:1 + 2 * twos:2], tallies[2:2 + 2 * twos:2]
    slack = jnp.minimum(donor - 1, reach - receiver)
    moved = jax.random.randint(jax.random.fold_in(own_key, 1), (twos,), 0, 1 << 20) % (slack + 1)
    tallies = tallies.at[1:1 + 2 * twos:2].set(donor - moved).at[2:2 + 2 * twos:2].set(receiver + moved)
    return tallies[jax.random.permutation(jax.random.fold_in(own_key, 2), amount)]


def gaussian(rng, dims, deviation, bound, split=(), held_as=jnp.bfloat16):
    values = jax.random.normal(rng, dims, jnp.float32) * deviation
    if len(split) > 0:
        values = block_scale(rng, dims, split, -0.22, 0.18) * values
    return jnp.clip(values, min=-bound, max=bound).astype(held_as)


def setup_inputs(seed: int = 0) -> dict:
    key_list = jax.random.split(jax.random.key(seed), 9)
    wavefunction = gaussian(key_list[0], (BOND, BOND), 1.0, 6.0, ((0, 64),))
    left_env = gaussian(key_list[1], (TERMS, SECTORS, CAP, CAP), (CAP * TERMS) ** -0.5, 0.1875, ((0, 8), (1, 64)))
    right_env = gaussian(key_list[2], (TERMS, SECTORS, CAP, CAP), CAP ** -0.5, 0.5, ((0, 8), (1, 64)))
    left_sizes = ragged(key_list[3], SECTORS, SECTORS * CAP * 3 // 4, CAP, 2).astype(jnp.int32)
    right_sizes = ragged(key_list[4], SECTORS, SECTORS * CAP * 3 // 4, CAP, 1).astype(jnp.int32)
    charge_left = set_ends(jax.random.randint(key_list[5], (SECTORS,), 0, 4), jax.random.fold_in(key_list[5], 1), 0, 3).astype(jnp.int32)
    charge_right = set_ends(jax.random.randint(key_list[6], (SECTORS,), 0, 4), jax.random.fold_in(key_list[6], 1), 0, 3).astype(jnp.int32)
    term_shift = set_ends(jax.random.randint(key_list[7], (TERMS,), -1, 2), jax.random.fold_in(key_list[7], 1), -1, 1).astype(jnp.int32)
    return {"wavefunction": wavefunction, "left_env": left_env, "right_env": right_env, "left_sizes": left_sizes, "right_sizes": right_sizes, "charge_left": charge_left, "charge_right": charge_right, "term_shift": term_shift}


def build_mask(left_sizes, right_sizes, charge_left, charge_right):
    place = jnp.arange(CAP, dtype=jnp.int32)
    row_ok = (place[None, :] < left_sizes[:, None]).reshape(-1)
    col_ok = (place[None, :] < right_sizes[:, None]).reshape(-1)
    pairs = jnp.abs(charge_left[:, None] - charge_right[None, :]) <= 1
    pairs = jnp.repeat(jnp.repeat(pairs, CAP, axis=0), CAP, axis=1)
    return (pairs & row_ok[:, None] & col_ok[None, :]).astype(jnp.bfloat16)


def reference(wavefunction, left_env, right_env, left_sizes, right_sizes, charge_left, charge_right, term_shift):
    allowed = build_mask(left_sizes, right_sizes, charge_left, charge_right)
    masked = wavefunction * allowed
    blocks = masked.reshape(SECTORS, CAP, SECTORS, CAP).astype(jnp.float32)
    zeros = jnp.zeros((SECTORS, CAP, SECTORS, CAP), jnp.float32)

    def one_term(carry, index):
        right_blocks = right_env[index].astype(jnp.float32)
        left_blocks = left_env[index].astype(jnp.float32)
        inner = jnp.einsum('aibj,bkj->aibk', blocks, right_blocks)
        inner = lax.optimization_barrier(inner.astype(jnp.bfloat16)).astype(jnp.float32)
        outer = jnp.einsum('aki,aibj->akbj', left_blocks, inner)
        shift_value = term_shift[index]
        stay, rise, fall = carry
        stay = stay + jnp.where(shift_value == 0, outer, 0.0)
        rise = rise + jnp.where(shift_value == 1, outer, 0.0)
        fall = fall + jnp.where(shift_value == -1, outer, 0.0)
        return (stay, rise, fall), None

    (stay, rise, fall), _ = lax.scan(one_term, (zeros, zeros, zeros), jnp.arange(TERMS, dtype=jnp.int32))
    rise = lax.optimization_barrier(rise.astype(jnp.bfloat16)).astype(jnp.float32)
    fall = lax.optimization_barrier(fall.astype(jnp.bfloat16)).astype(jnp.float32)
    edge = jnp.zeros((1, CAP, SECTORS, CAP), jnp.float32)
    total = stay + jnp.concatenate([edge, rise[:-1]], axis=0) + jnp.concatenate([fall[1:], edge], axis=0)
    total = total.reshape(BOND, BOND)
    return (total * allowed.astype(jnp.float32)).astype(jnp.bfloat16)
```

```python
import functools

import jax
import jax.numpy as jnp
from jax import lax
from jax.experimental import pallas as pl
from jax.experimental.pallas import tpu as pltpu
from jax.sharding import PartitionSpec as P

MESH = pl.DeviceIdType.MESH
LAG = 2


def kernel(
    nx,
    nz,
    block,
    wave,
    left,
    right,
    left_sizes,
    right_sizes,
    charge_left,
    charge_right,
    shift,
    out,
    rbuf,
    w3,
    l3,
    lcat,
    s1_send,
    s1_recv,
    z_send,
    z_recv,
    x_send,
    x_recv,
    w_send,
    w_recv,
    l_send,
    l_recv,
    g_send,
    g_recv,
):
    ny = nx
    half = nz // 2
    sectors = nx * nz
    terms = 2 * ny
    width = half * block
    s = lax.axis_index("sector")
    t = lax.axis_index("term")
    x = s // nz
    z = lax.rem(s, nz)
    y = t // 2
    c = lax.rem(t, 2)
    own = z // half == c
    own_j = lax.rem(z, half)
    kind = lax.rem(x, 2)
    mirror = jnp.logical_and(jnp.logical_and(own, x == y), c == kind)

    def dev(xx, yy, zz, cc):
        return (xx * nz + zz, yy * 2 + cc)

    x_next = dev(lax.rem(x + 1, nx), y, z, c)
    x_prev = dev(lax.rem(x + nx - 1, nx), y, z, c)
    z_next = dev(x, y, lax.rem(z + 1, nz), c)
    z_prev = dev(x, y, lax.rem(z + nz - 1, nz), c)
    s_next = (lax.rem(s + 1, sectors), t)
    s_prev = (lax.rem(s + sectors - 1, sectors), t)

    column = pl.multiple_of(t * width, 128)
    wave_own = wave.at[:, pl.ds(column, width)]
    left_own = left.at[0, 0]
    w_load = pltpu.make_async_copy(wave_own, w3.at[1], w_recv.at[1])
    l_load = pltpu.make_async_copy(left_own, l3.at[1], l_recv.at[1])
    l_load.start()
    w_load.start()

    barrier = pltpu.get_barrier_semaphore()

    def greet(target):
        pl.semaphore_signal(barrier, inc=1, device_id=target, device_id_type=MESH)

    @pl.when(own)
    def _():
        for yy in range(ny):
            source = dev(y, yy, z, kind)

            @pl.when(jnp.logical_not(jnp.logical_and(mirror, yy == y)))
            def _():
                greet(source)

    for target in (z_next, z_prev, x_next, x_prev, s_next, s_prev):
        greet(target)
    for step in range(1, terms):
        greet((s, lax.rem(t + step, terms)))
    pl.semaphore_wait(barrier, 6 + terms - 1 + nx // 2 - mirror.astype(jnp.int32))

    def remote(src, dst, send_sem, recv_sem, target):
        return pltpu.make_async_remote_copy(
            src_ref=src,
            dst_ref=dst,
            send_sem=send_sem,
            recv_sem=recv_sem,
            device_id=target,
            device_id_type=MESH,
        )

    right_own = right.at[0, 0]
    landing = rbuf.at[own_j, c * ny + y]
    first = [
        remote(right_own, landing, s1_send.at[m], s1_recv.at[y], dev(2 * m + c, x, z, z // half))
        for m in range(nx // 2)
    ]
    for m, copy in enumerate(first):
        itself = jnp.logical_and(mirror, 2 * m + c == x)

        @pl.when(jnp.logical_not(itself))
        def _():
            copy.start()

        @pl.when(itself)
        def _():
            pltpu.make_async_copy(right_own, landing, s1_recv.at[y]).start()

    l_up = remote(left_own, l3.at[0], l_send.at[0], l_recv.at[0], s_next)
    l_down = remote(left_own, l3.at[2], l_send.at[1], l_recv.at[2], s_prev)
    l_up.start()
    l_down.start()
    w_up = remote(wave_own, w3.at[0], w_send.at[0], w_recv.at[0], s_next)
    w_down = remote(wave_own, w3.at[2], w_send.at[1], w_recv.at[2], s_prev)
    w_up.start()
    w_down.start()

    def z_copy(j, sub, side):
        part = rbuf.at[j, pl.ds(kind * ny + sub * (ny // 2), ny // 2)]
        target = z_next if side == 0 else z_prev
        return remote(part, part, z_send.at[j, sub, side], z_recv.at[j, sub], target)

    def x_copy(j, sub):
        part = rbuf.at[j, pl.ds(kind * ny + sub * (ny // 2), ny // 2)]
        target = x_next if sub == 0 else x_prev
        return remote(part, part, x_send.at[j, sub], x_recv.at[j, sub], target)

    def x_wait(j, sub):
        part = rbuf.at[j, pl.ds((1 - kind) * ny + sub * (ny // 2), ny // 2)]
        target = x_next if sub == 0 else x_prev
        remote(part, part, x_send.at[j, sub], x_recv.at[j, sub], target).wait_recv()

    @pl.when(own)
    def _():
        for sub in range(2):
            for yy in range(sub * (ny // 2), (sub + 1) * (ny // 2)):
                block_in = rbuf.at[own_j, kind * ny + yy]
                remote(right_own, block_in, s1_send.at[0], s1_recv.at[yy], s_next).wait_recv()
            z_copy(own_j, sub, 0).start()
            z_copy(own_j, sub, 1).start()
            x_copy(own_j, sub).start()

    l_load.wait()
    l_up.wait_recv()
    l_down.wait_recv()
    place = pl.multiple_of(t * block, 128)
    lanes = pl.ds(place, block)
    lcat[0:block, lanes] = l3[1 - shift[0]]
    lcat[block : block + 16, lanes] = jnp.full((16, block), shift[0], jnp.int32).astype(
        jnp.float32
    ).astype(jnp.bfloat16)
    group = []
    for step in range(1, terms):
        copy = remote(
            lcat.at[:, lanes],
            lcat.at[:, lanes],
            g_send.at[step - 1],
            g_recv.at[t],
            (s, lax.rem(t + step, terms)),
        )
        copy.start()
        group.append(copy)

    def side_flags(k, sub, side):
        origin = lax.rem(z - k + nz if side == 0 else z + k, nz)
        active = origin // half == c
        j = lax.rem(origin, half)
        if sub == side:
            return j, active, jnp.logical_and(active, k < half)
        return (
            j,
            jnp.logical_and(active, k < half),
            jnp.logical_and(active, k < half - 1),
        )

    def move(k):
        for sub in range(2):
            for side in range(2):
                j, has, forward = side_flags(k, sub, side)

                @pl.when(has)
                def _():
                    z_copy(j, sub, side).wait_recv()

                    @pl.when(forward)
                    def _():
                        z_copy(j, sub, side).start()

                    x_copy(j, sub).start()

    def ready():
        w_load.wait()
        w_up.wait_recv()
        w_down.wait_recv()
        for step in range(1, terms):
            peer = lax.rem(t + step, terms)
            part = lcat.at[:, pl.ds(pl.multiple_of(peer * block, 128), block)]
            remote(part, part, g_send.at[0], g_recv.at[peer], s_next).wait_recv()

    row = lax.broadcasted_iota(jnp.int32, (block, block), 0)
    col = lax.broadcasted_iota(jnp.int32, (block, block), 1)

    def compute(j):
        for sub in range(2):
            x_wait(j, sub)
        b = y * nz + c * half + j
        at = pl.ds(pl.multiple_of(j * block, 128), block)
        masked = []
        for d in range(3):
            a = s + d - 1
            inside = jnp.logical_and(a >= 0, a < sectors)
            a = jnp.clip(a, 0, sectors - 1)
            pair = jnp.abs(charge_left[a] - charge_right[b]) <= 1
            rows = jnp.where(inside, left_sizes[a], 0)
            cols = jnp.where(pair, right_sizes[b], 0)
            keep = jnp.logical_and(row < rows, col < cols)
            if d == 1:
                keep_own = keep
            part = w3[d, :, at].astype(jnp.float32)
            masked.append(jnp.where(keep, part, 0.0).astype(jnp.bfloat16))
        inner = []
        for term in range(terms):
            slot = (term % 2) * ny + term // 2
            d = lcat[block : block + 16, term * block : (term + 1) * block].astype(jnp.float32)
            rise = (d * (d + 1.0) * 0.5).astype(jnp.bfloat16)
            fall = (d * (d - 1.0) * 0.5).astype(jnp.bfloat16)
            stay = (1.0 - d * d).astype(jnp.bfloat16)
            rise, fall, stay = (
                jnp.concatenate([m] * (block // 16), axis=0) for m in (rise, fall, stay)
            )
            chosen = masked[1] * stay + masked[0] * rise + masked[2] * fall
            inner.append(
                lax.dot_general(
                    chosen,
                    rbuf[j, slot],
                    (((1,), (1,)), ((), ())),
                    preferred_element_type=jnp.float32,
                ).astype(jnp.bfloat16)
            )
        stacked = jnp.concatenate(inner, axis=0)
        total = jnp.dot(lcat[0:block, :], stacked, preferred_element_type=jnp.float32)
        out[:, at] = jnp.where(keep_own, total, 0.0).astype(jnp.bfloat16)

    @pl.loop(1, half + LAG + 1)
    def _(k):
        @pl.when(k <= half)
        def _():
            move(k)

        @pl.when(k == LAG)
        def _():
            ready()

        @pl.loop(0, 2)
        def _(side):
            kk = k - LAG
            origin = lax.rem(z + nz + jnp.where(side == 0, -kk, kk), nz)
            once = jnp.logical_or(side == 0, jnp.logical_and(kk > 0, kk < half))

            @pl.when(
                jnp.logical_and(jnp.logical_and(kk >= 0, once), origin // half == c)
            )
            def _():
                compute(lax.rem(origin, half))

    for m, copy in enumerate(first):

        @pl.when(jnp.logical_not(jnp.logical_and(mirror, 2 * m + c == x)))
        def _():
            copy.wait_send()

    for copy in (l_up, l_down, w_up, w_down, *group):
        copy.wait_send()

    @pl.when(own)
    def _():
        for sub in range(2):
            z_copy(own_j, sub, 0).wait_send()
            z_copy(own_j, sub, 1).wait_send()

    @pl.loop(1, half)
    def _(k):
        for sub in range(2):
            for side in range(2):
                j, _, forward = side_flags(k, sub, side)

                @pl.when(forward)
                def _():
                    z_copy(j, sub, side).wait_send()

    @pl.loop(0, half)
    def _(j):
        for sub in range(2):
            x_copy(j, sub).wait_send()


def local(nx, nz, wave, left, right, left_sizes, right_sizes, charge_left, charge_right, shift):
    block = left.shape[2]
    half = nz // 2
    terms = 2 * nx
    width = half * block
    hbm = pl.BlockSpec(memory_space=pl.ANY)
    smem = pl.BlockSpec(memory_space=pltpu.SMEM)
    dma = pltpu.SemaphoreType.DMA
    return pl.pallas_call(
        functools.partial(kernel, nx, nz, block),
        out_shape=jax.ShapeDtypeStruct((block, width), jnp.bfloat16),
        in_specs=[hbm] * 3 + [smem] * 5,
        out_specs=pl.BlockSpec(memory_space=pltpu.VMEM),
        scratch_shapes=[
            pltpu.VMEM((half, terms, block, block), jnp.bfloat16),
            pltpu.VMEM((3, block, width), jnp.bfloat16),
            pltpu.VMEM((3, block, block), jnp.bfloat16),
            pltpu.VMEM((block + 16, terms * block), jnp.bfloat16),
            dma((nx // 2,)),
            dma((nx,)),
            dma((half, 2, 2)),
            dma((half, 2)),
            dma((half, 2)),
            dma((half, 2)),
            dma((2,)),
            dma((3,)),
            dma((2,)),
            dma((3,)),
            dma((terms - 1,)),
            dma((terms,)),
        ],
        compiler_params=pltpu.CompilerParams(
            collective_id=0, has_side_effects=True, vmem_limit_bytes=32 << 20
        ),
        cost_estimate=pl.CostEstimate(
            flops=4 * terms * half * block**3, bytes_accessed=1 << 20, transcendentals=0
        ),
    )(wave, left, right, left_sizes, right_sizes, charge_left, charge_right, shift)


def solution(mesh):
    sectors, terms = mesh.shape["sector"], mesh.shape["term"]
    nx = terms // 2
    placed = (
        P("sector", None),
        P("term", "sector", None, None),
        P("term", "sector", None, None),
        P(),
        P(),
        P(),
        P(),
        P("term"),
    )
    return jax.shard_map(
        functools.partial(local, nx, sectors // nx),
        mesh=mesh,
        in_specs=placed,
        out_specs=P("sector", "term"),
        check_vma=False,
    )
```

```python
import functools

import jax
import jax.numpy as jnp
from jax import lax
from jax.experimental import pallas as pl
from jax.experimental.pallas import tpu as pltpu
from jax.sharding import PartitionSpec as P

MESH = pl.DeviceIdType.MESH


def ring_plan(nz):
    stride = next(k for k in (5, 3) if nz == 3 * k + 1) if nz % 3 == 1 and nz > 4 else 0
    entries = (0, stride, nz - stride) if stride else (0,)
    reach = stride // 2 if stride else nz // 2 - 1
    steps = []
    for offset in range(nz):
        if offset == nz // 2:
            steps.append((reach + 1, offset, "both", (), ()))
            continue
        far = min(
            ((offset - e + nz // 2) % nz - nz // 2 for e in entries), key=lambda far: abs(far)
        )
        up = (0, 1) if 0 <= far < reach else ()
        down = (0, 1) if -reach < far <= 0 else ()
        if offset == nz // 2 - 1:
            up = (0,)
        if offset == nz // 2 + 1:
            down = (1,)
        side = "entry" if far == 0 else ("below" if far > 0 else "above")
        steps.append((abs(far), offset, side, up, down))
    return entries, sorted(steps)


def kernel(
    nx,
    nz,
    block,
    wave,
    left,
    right,
    left_sizes_in,
    right_sizes_in,
    charge_left_in,
    charge_right_in,
    shift_in,
    out,
    left_sizes,
    right_sizes,
    charge_left,
    charge_right,
    shift,
    scalar_sem,
    rbuf,
    w3,
    l3,
    lcat,
    s1_send,
    s1_recv,
    z_send,
    z_recv,
    x_send,
    x_recv,
    w_send,
    w_recv,
    l_send,
    l_recv,
    g_send,
    g_recv,
):
    ny = nx
    half = nz // 2
    sectors = nx * nz
    terms = 2 * ny
    width = half * block
    s = lax.axis_index("sector")
    t = lax.axis_index("term")
    x = s // nz
    z = lax.rem(s, nz)
    y = t // 2
    c = lax.rem(t, 2)
    kind = lax.rem(x, 2)
    entries, steps = ring_plan(nz)

    def meets(offset):
        origin = lax.rem(z - offset + nz, nz)
        return origin // half == c, lax.rem(origin, half)

    mirror = jnp.logical_and(jnp.logical_and(z // half == c, x == y), c == kind)

    def dev(xx, yy, zz, cc):
        return (xx * nz + zz, yy * 2 + cc)

    x_next = dev(lax.rem(x + 1, nx), y, z, c)
    x_prev = dev(lax.rem(x + nx - 1, nx), y, z, c)
    z_next = dev(x, y, lax.rem(z + 1, nz), c)
    z_prev = dev(x, y, lax.rem(z + nz - 1, nz), c)
    s_next = (lax.rem(s + 1, sectors), t)
    s_prev = (lax.rem(s + sectors - 1, sectors), t)

    column = pl.multiple_of(t * width, 128)
    wave_own = wave.at[:, pl.ds(column, width)]
    left_own = left.at[0, 0]
    w_load = pltpu.make_async_copy(wave_own, w3.at[1], w_recv.at[1])
    l_load = pltpu.make_async_copy(left_own, l3.at[1], l_recv.at[1])
    l_load.start()
    w_load.start()
    scalars = [
        pltpu.make_async_copy(source, held, scalar_sem.at[i])
        for i, (source, held) in enumerate(
            (
                (shift_in, shift),
                (left_sizes_in, left_sizes),
                (right_sizes_in, right_sizes),
                (charge_left_in, charge_left),
                (charge_right_in, charge_right),
            )
        )
    ]
    for copy in scalars:
        copy.start()

    barrier = pltpu.get_barrier_semaphore()

    def greet(target):
        pl.semaphore_signal(barrier, inc=1, device_id=target, device_id_type=MESH)

    for offset in entries:
        active, _ = meets(offset)
        for yy in range(ny):
            itself = jnp.logical_and(mirror, yy == y) if offset == 0 else False

            @pl.when(jnp.logical_and(active, jnp.logical_not(itself)))
            def _():
                greet(dev(y, yy, lax.rem(z - offset + nz, nz), kind))

    for target in (z_next, z_prev, x_next, x_prev, s_next, s_prev):
        greet(target)
    for step in range(1, terms):
        greet((s, lax.rem(t + step, terms)))
    pl.semaphore_wait(barrier, 6 + terms - 1 + len(entries) * (nx // 2) - mirror.astype(jnp.int32))

    def remote(src, dst, send_sem, recv_sem, target):
        return pltpu.make_async_remote_copy(
            src_ref=src,
            dst_ref=dst,
            send_sem=send_sem,
            recv_sem=recv_sem,
            device_id=target,
            device_id_type=MESH,
        )

    l_up = remote(left_own, l3.at[0], l_send.at[0], l_recv.at[0], s_next)
    l_down = remote(left_own, l3.at[2], l_send.at[1], l_recv.at[2], s_prev)
    l_up.start()
    l_down.start()

    right_own = right.at[0, 0]
    landing = rbuf.at[lax.rem(z, half), c * ny + y]
    landed = s1_recv.at[lax.rem(z, half), y]
    first = []
    for e, offset in enumerate(entries):
        for m in range(nx // 2):
            target = dev(2 * m + c, x, lax.rem(z + offset, nz), z // half)
            copy = remote(right_own, landing, s1_send.at[e, m], landed, target)
            itself = jnp.logical_and(mirror, 2 * m + c == x) if offset == 0 else None
            first.append((copy, itself))
            if itself is None:
                copy.start()
                continue

            @pl.when(jnp.logical_not(itself))
            def _():
                copy.start()

            @pl.when(itself)
            def _():
                pltpu.make_async_copy(right_own, landing, landed).start()

    w_up = remote(wave_own, w3.at[0], w_send.at[0], w_recv.at[0], s_next)
    w_down = remote(wave_own, w3.at[2], w_send.at[1], w_recv.at[2], s_prev)
    w_up.start()
    w_down.start()

    def z_copy(j, sub, side):
        part = rbuf.at[j, pl.ds(kind * ny + sub * (ny // 2), ny // 2)]
        target = z_next if side == 0 else z_prev
        return remote(part, part, z_send.at[j, sub, side], z_recv.at[j, sub], target)

    def x_copy(j, sub):
        part = rbuf.at[j, pl.ds(kind * ny + sub * (ny // 2), ny // 2)]
        target = x_next if sub == 0 else x_prev
        return remote(part, part, x_send.at[j, sub], x_recv.at[j, sub], target)

    def x_wait(j, sub):
        part = rbuf.at[j, pl.ds((1 - kind) * ny + sub * (ny // 2), ny // 2)]
        target = x_next if sub == 0 else x_prev
        remote(part, part, x_send.at[j, sub], x_recv.at[j, sub], target).wait_recv()

    scalars[0].wait()
    l_load.wait()
    l_up.wait_recv()
    l_down.wait_recv()
    place = pl.multiple_of(t * block, 128)
    lanes = pl.ds(place, block)
    lcat[0:block, lanes] = l3[1 - shift[0]]
    lcat[block : block + 16, lanes] = jnp.full((16, block), shift[0], jnp.int32).astype(
        jnp.float32
    ).astype(jnp.bfloat16)
    group = []
    for step in range(1, terms):
        copy = remote(
            lcat.at[:, lanes],
            lcat.at[:, lanes],
            g_send.at[step - 1],
            g_recv.at[t],
            (s, lax.rem(t + step, terms)),
        )
        copy.start()
        group.append(copy)

    def move(step):
        _, offset, side, up, down = step
        active, j = meets(offset)

        @pl.when(active)
        def _():
            for sub in range(2):
                if side == "entry":
                    for yy in range(sub * (ny // 2), (sub + 1) * (ny // 2)):
                        part = rbuf.at[j, kind * ny + yy]
                        remote(
                            right_own, part, s1_send.at[0, 0], s1_recv.at[j, yy], s_next
                        ).wait_recv()
                else:
                    z_copy(j, sub, 0).wait_recv()
                if sub in up:
                    z_copy(j, sub, 0).start()
                if sub in down:
                    z_copy(j, sub, 1).start()
                x_copy(j, sub).start()

    def ready():
        for copy in scalars[1:]:
            copy.wait()
        w_load.wait()
        w_up.wait_recv()
        w_down.wait_recv()
        for step in range(1, terms):
            peer = lax.rem(t + step, terms)
            part = lcat.at[:, pl.ds(pl.multiple_of(peer * block, 128), block)]
            remote(part, part, g_send.at[0], g_recv.at[peer], s_next).wait_recv()

    row = lax.broadcasted_iota(jnp.int32, (block, block), 0)
    col = lax.broadcasted_iota(jnp.int32, (block, block), 1)

    def compute(j):
        for sub in range(2):
            x_wait(j, sub)
        b = y * nz + c * half + j
        at = pl.ds(pl.multiple_of(j * block, 128), block)
        masked = []
        for d in range(3):
            a = s + d - 1
            inside = jnp.logical_and(a >= 0, a < sectors)
            a = jnp.clip(a, 0, sectors - 1)
            pair = jnp.abs(charge_left[a] - charge_right[b]) <= 1
            rows = jnp.where(inside, left_sizes[a], 0)
            cols = jnp.where(pair, right_sizes[b], 0)
            keep = jnp.logical_and(row < rows, col < cols)
            if d == 1:
                keep_own = keep
            part = w3[d, :, at].astype(jnp.float32)
            masked.append(jnp.where(keep, part, 0.0).astype(jnp.bfloat16))
        inner = []
        for term in range(terms):
            slot = (term % 2) * ny + term // 2
            d = lcat[block : block + 16, term * block : (term + 1) * block].astype(jnp.float32)
            rise = (d * (d + 1.0) * 0.5).astype(jnp.bfloat16)
            fall = (d * (d - 1.0) * 0.5).astype(jnp.bfloat16)
            stay = (1.0 - d * d).astype(jnp.bfloat16)
            rise, fall, stay = (
                jnp.concatenate([m] * (block // 16), axis=0) for m in (rise, fall, stay)
            )
            chosen = masked[1] * stay + masked[0] * rise + masked[2] * fall
            inner.append(
                lax.dot_general(
                    chosen,
                    rbuf[j, slot],
                    (((1,), (1,)), ((), ())),
                    preferred_element_type=jnp.float32,
                ).astype(jnp.bfloat16)
            )
        stacked = jnp.concatenate(inner, axis=0)
        total = jnp.dot(lcat[0:block, :], stacked, preferred_element_type=jnp.float32)
        out[:, at] = jnp.where(keep_own, total, 0.0).astype(jnp.bfloat16)

    for step in steps[:-1]:
        move(step)
    ready()

    @pl.loop(0, nz)
    def _(n):
        @pl.when(n == len(entries))
        def _():
            move(steps[-1])

        offset = functools.reduce(
            lambda found, i: jnp.where(n == i, steps[i][1], found), range(1, nz), steps[0][1]
        )
        active, j = meets(offset)

        @pl.when(active)
        def _():
            compute(j)

    for copy, itself in first:
        if itself is None:
            copy.wait_send()
            continue

        @pl.when(jnp.logical_not(itself))
        def _():
            copy.wait_send()

    for copy in (l_up, l_down, w_up, w_down, *group):
        copy.wait_send()

    for _, offset, _, up, down in steps:
        active, j = meets(offset)
        if not up + down:
            continue

        @pl.when(active)
        def _():
            for sub in up:
                z_copy(j, sub, 0).wait_send()
            for sub in down:
                z_copy(j, sub, 1).wait_send()

    @pl.loop(0, half)
    def _(j):
        for sub in range(2):
            x_copy(j, sub).wait_send()


def local(nx, nz, wave, left, right, left_sizes, right_sizes, charge_left, charge_right, shift):
    block = left.shape[2]
    half = nz // 2
    terms = 2 * nx
    width = half * block
    hbm = pl.BlockSpec(memory_space=pl.ANY)
    sectors = nx * nz
    entries, _ = ring_plan(nz)
    dma = pltpu.SemaphoreType.DMA
    return pl.pallas_call(
        functools.partial(kernel, nx, nz, block),
        out_shape=jax.ShapeDtypeStruct((block, width), jnp.bfloat16),
        in_specs=[hbm] * 8,
        out_specs=pl.BlockSpec(memory_space=pltpu.VMEM),
        scratch_shapes=[
            pltpu.SMEM((sectors,), jnp.int32),
            pltpu.SMEM((sectors,), jnp.int32),
            pltpu.SMEM((sectors,), jnp.int32),
            pltpu.SMEM((sectors,), jnp.int32),
            pltpu.SMEM((1,), jnp.int32),
            dma((5,)),
            pltpu.VMEM((half, terms, block, block), jnp.bfloat16),
            pltpu.VMEM((3, block, width), jnp.bfloat16),
            pltpu.VMEM((3, block, block), jnp.bfloat16),
            pltpu.VMEM((block + 16, terms * block), jnp.bfloat16),
            dma((len(entries), nx // 2)),
            dma((half, nx)),
            dma((half, 2, 2)),
            dma((half, 2)),
            dma((half, 2)),
            dma((half, 2)),
            dma((2,)),
            dma((3,)),
            dma((2,)),
            dma((3,)),
            dma((terms - 1,)),
            dma((terms,)),
        ],
        compiler_params=pltpu.CompilerParams(
            collective_id=0, has_side_effects=True, vmem_limit_bytes=60 << 20
        ),
        cost_estimate=pl.CostEstimate(
            flops=4 * terms * half * block**3, bytes_accessed=1 << 20, transcendentals=0
        ),
    )(wave, left, right, left_sizes, right_sizes, charge_left, charge_right, shift)


def solution(mesh):
    sectors, terms = mesh.shape["sector"], mesh.shape["term"]
    nx = terms // 2
    placed = (
        P("sector", None),
        P("term", "sector", None, None),
        P("term", "sector", None, None),
        P(),
        P(),
        P(),
        P(),
        P("term"),
    )
    return jax.shard_map(
        functools.partial(local, nx, sectors // nx),
        mesh=mesh,
        in_specs=placed,
        out_specs=P("sector", "term"),
        check_vma=False,
    )
```

```python
import functools

import jax
import jax.numpy as jnp
from jax import lax
from jax.experimental import pallas as pl
from jax.experimental.pallas import tpu as pltpu
from jax.sharding import PartitionSpec as P

MESH = pl.DeviceIdType.MESH
PIECES = 4


def ring_plan(nz):
    entries = (0, 5, 11) if nz == 16 else (0, 3, 7) if nz == 10 else (0,)
    middle = nz // 2
    near = max(e for e in entries if e < middle)

    def comes(offset):
        if offset == middle:
            return 1.5, 0
        below = min((offset - e) % nz for e in entries)
        above = min((e - offset) % nz for e in entries)
        return (0, 0) if below == 0 else (below, 1) if below < above else (above, -1)

    depths = []
    for depth in sorted({comes(offset)[0] for offset in range(nz)}):
        have = [offset for offset in range(nz) if comes(offset)[0] == depth]
        up = [offset for offset in have if comes((offset + 1) % nz)[1] == 1]
        down = [offset for offset in have if comes((offset - 1) % nz)[1] == -1]
        jump_up = [offset for offset in have if offset == near]
        jump_down = [offset for offset in have if offset == (nz - near) % nz]
        depths.append((have, up, down, (jump_up, jump_down)))
    return entries, middle - near, depths


def one_of(value, choices):
    return functools.reduce(jnp.logical_or, [value == choice for choice in choices])


def kernel(
    nx,
    nz,
    block,
    wave,
    left,
    right,
    left_sizes_in,
    right_sizes_in,
    charge_left_in,
    charge_right_in,
    shift_in,
    out,
    left_sizes,
    right_sizes,
    charge_left,
    charge_right,
    shift,
    scalar_sem,
    rbuf,
    w3,
    l3,
    lbuf,
    mw,
    inner,
    obuf,
    s1_send,
    s1_recv,
    z_send,
    z_recv,
    jump_send,
    w_send,
    w_recv,
    l_send,
    l_recv,
    lx_send,
    lx_recv,
    ly_send,
    ly_recv,
    sib_send,
    sib_recv,
    o_send,
    o_recv,
):
    ny = nx
    half = nz // 2
    share = half // nx
    sectors = nx * nz
    terms = 2 * ny
    width = half * block
    part_width = share * block
    s = lax.axis_index("sector")
    t = lax.axis_index("term")
    x = s // nz
    z = lax.rem(s, nz)
    y = t // 2
    c = lax.rem(t, 2)
    entries, jump, depths = ring_plan(nz)

    def dev(xx, yy, zz, cc):
        return (xx * nz + zz, yy * 2 + cc)

    def along(value, step, size):
        return lax.rem(value + step + size, size)

    origins = [c * half + x * share + q for q in range(share)]
    roles = [lax.rem(z - origin + nz, nz) for origin in origins]
    above, below = along(z, 1, nz), along(z, -1, nz)
    z_sides = (dev(x, y, above, c), dev(x, y, below, c))
    z_jumps = (dev(x, y, along(z, jump, nz), c), dev(x, y, along(z, -jump, nz), c))
    sibling = (s, t + 1 - 2 * c)
    s_next, s_prev = lax.rem(s + 1, sectors), lax.rem(s + sectors - 1, sectors)

    ring_x, ring_c = lax.rem(z, half) // share, z // half
    mirror = jnp.logical_and(jnp.logical_and(ring_x == x, x == y), ring_c == c)

    def columns(xx):
        start = pl.multiple_of(t * width + xx * part_width, 128)
        return wave.at[:, pl.ds(start, part_width)]

    left_own = left.at[0, 0]
    w_load = pltpu.make_async_copy(columns(x), w3.at[1, x], w_recv.at[1, x])
    l_load = pltpu.make_async_copy(left_own, l3.at[1], l_recv.at[1])
    l_load.start()
    w_load.start()
    scalars = [
        pltpu.make_async_copy(source, held, scalar_sem.at[i])
        for i, (source, held) in enumerate(
            (
                (shift_in, shift),
                (left_sizes_in, left_sizes),
                (right_sizes_in, right_sizes),
                (charge_left_in, charge_left),
                (charge_right_in, charge_right),
            )
        )
    ]
    for copy in scalars:
        copy.start()

    barrier = pltpu.get_barrier_semaphore()

    def greet(target):
        pl.semaphore_signal(barrier, inc=1, device_id=target, device_id_type=MESH)

    for q in range(share):

        @pl.when(one_of(roles[q], entries))
        def _():
            for yy in range(ny):
                for cc in range(2):
                    itself = jnp.logical_and(
                        jnp.logical_and(x == y, z == origins[q]),
                        jnp.logical_and(yy == y, cc == c),
                    )

                    @pl.when(jnp.logical_not(itself))
                    def _():
                        greet(dev(y, yy, origins[q], cc))

    for xx in range(nx):
        greet(dev(xx, y, above, c))
        greet(dev(xx, y, below, c))
    for target in (*z_jumps, sibling):
        greet(target)
    for k in range(1, nx):
        greet(dev(along(x, k, nx), y, z, c))
        greet(dev(x, along(y, k, ny), z, c))
    partners = 2 * nx + 3 + 2 * (nx - 1)
    pl.semaphore_wait(barrier, partners + len(entries) - mirror.astype(jnp.int32))

    def remote(src, dst, send_sem, recv_sem, target):
        return pltpu.make_async_remote_copy(
            src_ref=src,
            dst_ref=dst,
            send_sem=send_sem,
            recv_sem=recv_sem,
            device_id=target,
            device_id_type=MESH,
        )

    l_up = remote(left_own, l3.at[0], l_send.at[0], l_recv.at[0], (s_next, t))
    l_down = remote(left_own, l3.at[2], l_send.at[1], l_recv.at[2], (s_prev, t))
    l_up.start()
    l_down.start()

    right_own = right.at[0, 0]
    own_q = lax.rem(z, share)
    landing, landed = rbuf.at[own_q, t], s1_recv.at[own_q, t]
    first = [
        remote(right_own, landing, s1_send.at[e], landed, dev(ring_x, x, along(z, off, nz), ring_c))
        for e, off in enumerate(entries)
    ]
    for copy in first[1:]:
        copy.start()

    @pl.when(mirror)
    def _():
        pltpu.make_async_copy(right_own, landing, landed).start()

    @pl.when(jnp.logical_not(mirror))
    def _():
        first[0].start()

    waves = []
    for d, row_to in ((0, s_next), (2, s_prev)):
        for xx in range(nx):
            target = dev(xx, y, lax.rem(row_to, nz), c)
            dst = w3.at[d, row_to // nz]
            waves.append(
                remote(columns(xx), dst, w_send.at[d, xx], w_recv.at[d, row_to // nz], target)
            )
    for k in range(1, nx):
        xx = along(x, k, nx)
        waves.append(
            remote(columns(xx), w3.at[1, x], w_send.at[1, k], w_recv.at[1, x], dev(xx, y, z, c))
        )

    scalars[0].wait()
    l_load.wait()
    l_up.wait_recv()
    l_down.wait_recv()
    lbuf[c, y, x, 0:block, :] = l3[1 - shift[0]]
    lbuf[c, y, x, block : block + 16, :] = (
        jnp.full((16, block), shift[0], jnp.int32).astype(jnp.float32).astype(jnp.bfloat16)
    )

    def along_x(k, of):
        part = lbuf.at[c, y, of]
        target = dev(along(x, k, nx), y, z, c)
        return remote(part, part, lx_send.at[k - 1], lx_recv.at[k - 1], target)

    def along_y(k, of):
        part = lbuf.at[c, of]
        target = dev(x, along(y, k, ny), z, c)
        return remote(part, part, ly_send.at[k - 1], ly_recv.at[k - 1], target)

    def to_sibling(k, of, core):
        part = lbuf.at[core, of]
        return remote(part, part, sib_send.at[k], sib_recv.at[k], sibling)

    for k in range(1, nx):
        along_x(k, x).start()

    blocks = terms // PIECES

    def z_part(q, sub):
        return rbuf.at[q, pl.ds(sub * blocks, blocks)]

    def z_copy(q, sub, side):
        part = z_part(q, sub)
        return remote(part, part, z_send.at[q, sub, side], z_recv.at[q, sub], z_sides[side])

    def z_jump(q, sub):
        part = z_part(q, sub)
        return remote(part, part, jump_send.at[q, sub], z_recv.at[q, sub], z_jumps[2 * sub // PIECES])

    def when_role(q, offsets, act):
        if offsets:
            pl.when(one_of(roles[q], offsets))(act)

    for have, up, down, jumps in depths:
        for q in range(share):

            def pass_on(q=q, have=have, up=up, down=down, jumps=jumps):
                for sub in range(PIECES):
                    if have[0] in entries:
                        for k in range(sub * blocks, (sub + 1) * blocks):
                            copy = remote(
                                right_own, rbuf.at[q, k], s1_send.at[0], s1_recv.at[q, k], sibling
                            )
                            copy.wait_recv()
                    else:
                        z_copy(q, sub, 0).wait_recv()
                    when_role(q, jumps[2 * sub // PIECES], lambda: z_jump(q, sub).start())
                    when_role(q, up, lambda: z_copy(q, sub, 0).start())
                    when_role(q, down, lambda: z_copy(q, sub, 1).start())

            when_role(q, have, pass_on)
        if have[0] in entries:
            for k in range(1, nx):
                along_x(k, along(x, -k, nx)).wait_recv()
            for k in range(1, ny):
                along_y(k, y).start()
            to_sibling(0, y, c).start()
            for copy in waves:
                copy.start()

    for k in range(1, ny):
        of = along(y, -k, ny)
        along_y(k, of).wait_recv()
        to_sibling(k, of, c).start()
    for copy in scalars[1:]:
        copy.wait()
    w_load.wait()
    for d in range(3):
        for k in range(nx):
            of = along(x, k, nx)
            if d == 1 and k == 0:
                continue
            part = w3.at[d, of]
            remote(part, part, w_send.at[d, 0], w_recv.at[d, of], sibling).wait_recv()
    for k in range(ny):
        to_sibling(k, along(y, -k, ny), 1 - c).wait_recv()

    row = lax.broadcasted_iota(jnp.int32, (block, block), 0)
    col = lax.broadcasted_iota(jnp.int32, (block, block), 1)

    def allowed(a, b):
        inside = jnp.logical_and(a >= 0, a < sectors)
        a = jnp.clip(a, 0, sectors - 1)
        pair = jnp.abs(charge_left[a] - charge_right[b]) <= 1
        rows = jnp.where(inside, left_sizes[a], 0)
        cols = jnp.where(pair, right_sizes[b], 0)
        return jnp.logical_and(row < rows, col < cols)

    def ship(q, k, of):
        xx = along(x, k, nx)
        place = pl.multiple_of(of * part_width + q * block, 128)
        dst = out.at[:, pl.ds(place, block)]
        return remote(
            obuf.at[q, xx], dst, o_send.at[q, k - 1], o_recv.at[q, k - 1], dev(xx, y, z, c)
        )

    @pl.loop(0, share)
    def _(q):
        b = y * nz + c * half + x * share + q
        at = pl.ds(pl.multiple_of(q * block, 128), block)
        for xx in range(nx):
            for d in range(3):
                part = w3[d, xx, :, at].astype(jnp.float32)
                keep = allowed(nz * xx + z + d - 1, b)
                mw[d, xx * block : (xx + 1) * block, :] = jnp.where(keep, part, 0.0).astype(
                    jnp.bfloat16
                )
        for term in range(terms):
            d = lbuf[term % 2, term // 2, 0, block : block + 16, :].astype(jnp.float32)
            rise = (d * (d + 1.0) * 0.5).astype(jnp.bfloat16)
            fall = (d * (d - 1.0) * 0.5).astype(jnp.bfloat16)
            stay = (1.0 - d * d).astype(jnp.bfloat16)
            rise, fall, stay = (
                jnp.concatenate([m] * (nx * block // 16), axis=0) for m in (rise, fall, stay)
            )
            chosen = mw[1] * stay + mw[0] * rise + mw[2] * fall
            product = lax.dot_general(
                chosen, rbuf[q, term], (((1,), (1,)), ((), ())), preferred_element_type=jnp.float32
            ).astype(jnp.bfloat16)
            for xx in range(nx):
                inner[xx, term * block : (term + 1) * block, :] = product[
                    xx * block : (xx + 1) * block
                ]
        for xx in range(nx):
            lefts = jnp.concatenate(
                [lbuf[term % 2, term // 2, xx, 0:block, :] for term in range(terms)], axis=1
            )
            total = jnp.dot(lefts, inner[xx], preferred_element_type=jnp.float32)
            keep = allowed(nz * xx + z, b)
            obuf[q, xx] = jnp.where(keep, total, 0.0).astype(jnp.bfloat16)
        for k in range(1, nx):
            ship(q, k, x).start()
        place = pl.multiple_of(x * part_width + q * block, 128)
        out[:, pl.ds(place, block)] = obuf[q, x]

    for copy in first[1:]:
        copy.wait_send()

    @pl.when(jnp.logical_not(mirror))
    def _():
        first[0].wait_send()

    for copy in (l_up, l_down, *waves):
        copy.wait_send()
    for k in range(1, nx):
        along_x(k, x).wait_send()
        along_y(k, y).wait_send()
    to_sibling(0, y, c).wait_send()
    for k in range(1, ny):
        to_sibling(k, along(y, -k, ny), c).wait_send()
    for _, up, down, jumps in depths:
        for q in range(share):
            for sub in range(PIECES):
                when_role(q, jumps[2 * sub // PIECES], lambda: z_jump(q, sub).wait_send())
                when_role(q, up, lambda: z_copy(q, sub, 0).wait_send())
                when_role(q, down, lambda: z_copy(q, sub, 1).wait_send())
    for q in range(share):
        for k in range(1, nx):
            ship(q, k, x).wait_send()
            ship(q, k, along(x, -k, nx)).wait_recv()


def local(nx, nz, wave, left, right, left_sizes, right_sizes, charge_left, charge_right, shift):
    block = left.shape[2]
    ny = nx
    half = nz // 2
    share = half // nx
    terms = 2 * ny
    sectors = nx * nz
    entries, _, _ = ring_plan(nz)
    hbm = pl.BlockSpec(memory_space=pl.ANY)
    dma = pltpu.SemaphoreType.DMA
    half_float = jnp.bfloat16
    return pl.pallas_call(
        functools.partial(kernel, nx, nz, block),
        out_shape=jax.ShapeDtypeStruct((block, half * block), jnp.bfloat16),
        in_specs=[hbm] * 8,
        out_specs=pl.BlockSpec(memory_space=pltpu.VMEM),
        scratch_shapes=[
            pltpu.SMEM((sectors,), jnp.int32),
            pltpu.SMEM((sectors,), jnp.int32),
            pltpu.SMEM((sectors,), jnp.int32),
            pltpu.SMEM((sectors,), jnp.int32),
            pltpu.SMEM((1,), jnp.int32),
            dma((5,)),
            pltpu.VMEM((share, terms, block, block), half_float),
            pltpu.VMEM((3, nx, block, share * block), half_float),
            pltpu.VMEM((3, block, block), half_float),
            pltpu.VMEM((2, ny, nx, block + 16, block), half_float),
            pltpu.VMEM((3, nx * block, block), half_float),
            pltpu.VMEM((nx, terms * block, block), half_float),
            pltpu.VMEM((share, nx, block, block), half_float),
            dma((len(entries),)),
            dma((share, terms)),
            dma((share, PIECES, 2)),
            dma((share, PIECES)),
            dma((share, PIECES)),
            dma((3, nx)),
            dma((3, nx)),
            dma((2,)),
            dma((3,)),
            dma((nx - 1,)),
            dma((nx - 1,)),
            dma((ny - 1,)),
            dma((ny - 1,)),
            dma((ny,)),
            dma((ny,)),
            dma((share, nx - 1)),
            dma((share, nx - 1)),
        ],
        compiler_params=pltpu.CompilerParams(
            collective_id=0, has_side_effects=True, vmem_limit_bytes=60 << 20
        ),
        cost_estimate=pl.CostEstimate(
            flops=4 * terms * half * block**3, bytes_accessed=1 << 20, transcendentals=0
        ),
    )(wave, left, right, left_sizes, right_sizes, charge_left, charge_right, shift)


def solution(mesh):
    sectors, terms = mesh.shape["sector"], mesh.shape["term"]
    nx = terms // 2
    placed = (
        P("sector", None),
        P("term", "sector", None, None),
        P("term", "sector", None, None),
        P(),
        P(),
        P(),
        P(),
        P("term"),
    )
    return jax.shard_map(
        functools.partial(local, nx, sectors // nx),
        mesh=mesh,
        in_specs=placed,
        out_specs=P("sector", "term"),
        check_vma=False,
    )
```

```python
import functools

import jax
import jax.numpy as jnp
from jax import lax
from jax.experimental import pallas as pl
from jax.experimental.pallas import tpu as pltpu
from jax.sharding import PartitionSpec as P

MESH = pl.DeviceIdType.MESH
PIECES = 4


def ring_plan(nz):
    entries = (0, 5, 11) if nz == 16 else (0, 3, 7) if nz == 10 else (0,)
    middle = nz // 2
    near = middle - 1

    def comes(offset):
        if offset == middle:
            return nz, 0
        below = min((offset - e) % nz for e in entries)
        above = min((e - offset) % nz for e in entries)
        return (0, 0) if below == 0 else (below, 1) if below < above else (above, -1)

    depths = []
    for depth in sorted({comes(offset)[0] for offset in range(nz)}):
        have = [offset for offset in range(nz) if comes(offset)[0] == depth]
        up = [offset for offset in have if comes((offset + 1) % nz)[1] == 1]
        down = [offset for offset in have if comes((offset - 1) % nz)[1] == -1]
        jump_up = [offset for offset in have if offset == near]
        jump_down = [offset for offset in have if offset == (nz - near) % nz]
        depths.append((have, up, down, (jump_up, jump_down)))
    return entries, middle - near, depths


def one_of(value, choices):
    return functools.reduce(jnp.logical_or, [value == choice for choice in choices])


def kernel(
    nx,
    nz,
    block,
    wave,
    left,
    right,
    left_sizes_in,
    right_sizes_in,
    charge_left_in,
    charge_right_in,
    shift_in,
    out,
    left_sizes,
    right_sizes,
    charge_left,
    charge_right,
    shift,
    scalar_sem,
    rbuf,
    w3,
    l3,
    lbuf,
    mw,
    inner,
    obuf,
    s1_send,
    s1_recv,
    z_send,
    z_recv,
    jump_send,
    w_send,
    w_recv,
    l_send,
    l_recv,
    lx_send,
    lx_recv,
    ly_send,
    ly_recv,
    sib_send,
    sib_recv,
    o_send,
    o_recv,
):
    ny = nx
    half = nz // 2
    share = half // nx
    sectors = nx * nz
    terms = 2 * ny
    width = half * block
    part_width = share * block
    s = lax.axis_index("sector")
    t = lax.axis_index("term")
    x = s // nz
    z = lax.rem(s, nz)
    y = t // 2
    c = lax.rem(t, 2)
    entries, jump, depths = ring_plan(nz)

    def dev(xx, yy, zz, cc):
        return (xx * nz + zz, yy * 2 + cc)

    def along(value, step, size):
        return lax.rem(value + step + size, size)

    origins = [c * half + x * share + q for q in range(share)]
    roles = [lax.rem(z - origin + nz, nz) for origin in origins]
    above, below = along(z, 1, nz), along(z, -1, nz)
    z_sides = (dev(x, y, above, c), dev(x, y, below, c))
    z_jumps = (dev(x, y, along(z, jump, nz), c), dev(x, y, along(z, -jump, nz), c))
    sibling = (s, t + 1 - 2 * c)
    s_next, s_prev = lax.rem(s + 1, sectors), lax.rem(s + sectors - 1, sectors)

    ring_x, ring_c = lax.rem(z, half) // share, z // half
    mirror = jnp.logical_and(jnp.logical_and(ring_x == x, x == y), ring_c == c)

    def columns(xx):
        start = pl.multiple_of(t * width + xx * part_width, 128)
        return wave.at[:, pl.ds(start, part_width)]

    left_own = left.at[0, 0]
    w_load = pltpu.make_async_copy(columns(x), w3.at[1, x], w_recv.at[1, x])
    l_load = pltpu.make_async_copy(left_own, l3.at[1], l_recv.at[1])
    l_load.start()
    w_load.start()
    scalars = [
        pltpu.make_async_copy(source, held, scalar_sem.at[i])
        for i, (source, held) in enumerate(
            (
                (shift_in, shift),
                (left_sizes_in, left_sizes),
                (right_sizes_in, right_sizes),
                (charge_left_in, charge_left),
                (charge_right_in, charge_right),
            )
        )
    ]
    for copy in scalars:
        copy.start()

    barrier = pltpu.get_barrier_semaphore()

    def greet(target):
        pl.semaphore_signal(barrier, inc=1, device_id=target, device_id_type=MESH)

    for q in range(share):

        @pl.when(one_of(roles[q], entries))
        def _():
            for yy in range(ny):
                for cc in range(2):
                    itself = jnp.logical_and(
                        jnp.logical_and(x == y, z == origins[q]),
                        jnp.logical_and(yy == y, cc == c),
                    )

                    @pl.when(jnp.logical_not(itself))
                    def _():
                        greet(dev(y, yy, origins[q], cc))

    for xx in range(nx):
        greet(dev(xx, y, above, c))
        greet(dev(xx, y, below, c))
    for target in (*z_jumps, sibling):
        greet(target)
    for k in range(1, nx):
        greet(dev(along(x, k, nx), y, z, c))
        greet(dev(x, along(y, k, ny), z, c))
    partners = 2 * nx + 3 + 2 * (nx - 1)
    pl.semaphore_wait(barrier, partners + len(entries) - mirror.astype(jnp.int32))

    def remote(src, dst, send_sem, recv_sem, target):
        return pltpu.make_async_remote_copy(
            src_ref=src,
            dst_ref=dst,
            send_sem=send_sem,
            recv_sem=recv_sem,
            device_id=target,
            device_id_type=MESH,
        )

    l_up = remote(left_own, l3.at[0], l_send.at[0], l_recv.at[0], (s_next, t))
    l_down = remote(left_own, l3.at[2], l_send.at[1], l_recv.at[2], (s_prev, t))
    l_up.start()
    l_down.start()

    right_own = right.at[0, 0]
    own_q = lax.rem(z, share)
    landing, landed = rbuf.at[own_q, t], s1_recv.at[own_q, t]
    first = [
        remote(right_own, landing, s1_send.at[e], landed, dev(ring_x, x, along(z, off, nz), ring_c))
        for e, off in enumerate(entries)
    ]
    for copy in first[1:]:
        copy.start()

    @pl.when(mirror)
    def _():
        pltpu.make_async_copy(right_own, landing, landed).start()

    @pl.when(jnp.logical_not(mirror))
    def _():
        first[0].start()

    waves = []
    for d, row_to in ((0, s_next), (2, s_prev)):
        for xx in range(nx):
            target = dev(xx, y, lax.rem(row_to, nz), c)
            dst = w3.at[d, row_to // nz]
            waves.append(
                remote(columns(xx), dst, w_send.at[d, xx], w_recv.at[d, row_to // nz], target)
            )
    for k in range(1, nx):
        xx = along(x, k, nx)
        waves.append(
            remote(columns(xx), w3.at[1, x], w_send.at[1, k], w_recv.at[1, x], dev(xx, y, z, c))
        )

    scalars[0].wait()
    l_load.wait()
    l_up.wait_recv()
    l_down.wait_recv()
    lbuf[c, y, x, 0:block, :] = l3[1 - shift[0]]
    lbuf[c, y, x, block : block + 16, :] = (
        jnp.full((16, block), shift[0], jnp.int32).astype(jnp.float32).astype(jnp.bfloat16)
    )

    def along_x(k, of):
        part = lbuf.at[c, y, of]
        target = dev(along(x, k, nx), y, z, c)
        return remote(part, part, lx_send.at[k - 1], lx_recv.at[k - 1], target)

    def along_y(k, of):
        part = lbuf.at[c, of]
        target = dev(x, along(y, k, ny), z, c)
        return remote(part, part, ly_send.at[k - 1], ly_recv.at[k - 1], target)

    def to_sibling(k, of, core):
        part = lbuf.at[core, of]
        return remote(part, part, sib_send.at[k], sib_recv.at[k], sibling)

    for k in range(1, nx):
        along_x(k, x).start()
    for copy in waves[: 2 * nx]:
        copy.start()

    blocks = terms // PIECES

    def z_part(q, sub):
        return rbuf.at[q, pl.ds(sub * blocks, blocks)]

    def z_copy(q, sub, side):
        part = z_part(q, sub)
        return remote(part, part, z_send.at[q, sub, side], z_recv.at[q, sub], z_sides[side])

    def z_jump(q, sub):
        part = z_part(q, sub)
        return remote(part, part, jump_send.at[q, sub], z_recv.at[q, sub], z_jumps[2 * sub // PIECES])

    def when_role(q, offsets, act):
        if offsets:
            pl.when(one_of(roles[q], offsets))(act)

    for have, up, down, jumps in depths:
        for q in range(share):

            def pass_on(q=q, have=have, up=up, down=down, jumps=jumps):
                for sub in range(PIECES):
                    if have[0] in entries:
                        for k in range(sub * blocks, (sub + 1) * blocks):
                            copy = remote(
                                right_own, rbuf.at[q, k], s1_send.at[0], s1_recv.at[q, k], sibling
                            )
                            copy.wait_recv()
                    else:
                        z_copy(q, sub, 0).wait_recv()
                    when_role(q, jumps[2 * sub // PIECES], lambda: z_jump(q, sub).start())
                    when_role(q, up, lambda: z_copy(q, sub, 0).start())
                    when_role(q, down, lambda: z_copy(q, sub, 1).start())

            when_role(q, have, pass_on)
        if have is depths[min(2, len(depths) - 1)][0]:
            for k in range(1, ny):
                of = along(y, -k, ny)
                along_y(k, of).wait_recv()
                to_sibling(k, of, c).start()
        if have[0] in entries:
            for k in range(1, nx):
                along_x(k, along(x, -k, nx)).wait_recv()
            for k in range(1, ny):
                along_y(k, y).start()
            to_sibling(0, y, c).start()
            for copy in waves[2 * nx :]:
                copy.start()

    for copy in scalars[1:]:
        copy.wait()
    w_load.wait()
    for d in range(3):
        for k in range(nx):
            of = along(x, k, nx)
            if d == 1 and k == 0:
                continue
            part = w3.at[d, of]
            remote(part, part, w_send.at[d, 0], w_recv.at[d, of], sibling).wait_recv()
    for k in range(ny):
        to_sibling(k, along(y, -k, ny), 1 - c).wait_recv()

    row = lax.broadcasted_iota(jnp.int32, (block, block), 0)
    col = lax.broadcasted_iota(jnp.int32, (block, block), 1)

    def allowed(a, b):
        inside = jnp.logical_and(a >= 0, a < sectors)
        a = jnp.clip(a, 0, sectors - 1)
        pair = jnp.abs(charge_left[a] - charge_right[b]) <= 1
        rows = jnp.where(inside, left_sizes[a], 0)
        cols = jnp.where(pair, right_sizes[b], 0)
        return jnp.logical_and(row < rows, col < cols)

    def ship(q, k, of):
        xx = along(x, k, nx)
        place = pl.multiple_of(of * part_width + q * block, 128)
        dst = out.at[:, pl.ds(place, block)]
        return remote(
            obuf.at[q, xx], dst, o_send.at[q, k - 1], o_recv.at[q, k - 1], dev(xx, y, z, c)
        )

    @pl.loop(0, share)
    def _(q):
        b = y * nz + c * half + x * share + q
        at = pl.ds(pl.multiple_of(q * block, 128), block)
        for xx in range(nx):
            for d in range(3):
                part = w3[d, xx, :, at].astype(jnp.float32)
                keep = allowed(nz * xx + z + d - 1, b)
                mw[d, xx * block : (xx + 1) * block, :] = jnp.where(keep, part, 0.0).astype(
                    jnp.bfloat16
                )
        for term in range(terms):
            d = lbuf[term % 2, term // 2, 0, block : block + 16, :].astype(jnp.float32)
            rise = (d * (d + 1.0) * 0.5).astype(jnp.bfloat16)
            fall = (d * (d - 1.0) * 0.5).astype(jnp.bfloat16)
            stay = (1.0 - d * d).astype(jnp.bfloat16)
            rise, fall, stay = (
                jnp.concatenate([m] * (nx * block // 16), axis=0) for m in (rise, fall, stay)
            )
            chosen = mw[1] * stay + mw[0] * rise + mw[2] * fall
            product = lax.dot_general(
                chosen, rbuf[q, term], (((1,), (1,)), ((), ())), preferred_element_type=jnp.float32
            ).astype(jnp.bfloat16)
            for xx in range(nx):
                inner[xx, term * block : (term + 1) * block, :] = product[
                    xx * block : (xx + 1) * block
                ]
        for xx in range(nx):
            lefts = jnp.concatenate(
                [lbuf[term % 2, term // 2, xx, 0:block, :] for term in range(terms)], axis=1
            )
            total = jnp.dot(lefts, inner[xx], preferred_element_type=jnp.float32)
            keep = allowed(nz * xx + z, b)
            obuf[q, xx] = jnp.where(keep, total, 0.0).astype(jnp.bfloat16)
        for k in range(1, nx):
            ship(q, k, x).start()
        place = pl.multiple_of(x * part_width + q * block, 128)
        out[:, pl.ds(place, block)] = obuf[q, x]

    for copy in first[1:]:
        copy.wait_send()

    @pl.when(jnp.logical_not(mirror))
    def _():
        first[0].wait_send()

    for copy in (l_up, l_down, *waves):
        copy.wait_send()
    for k in range(1, nx):
        along_x(k, x).wait_send()
        along_y(k, y).wait_send()
    to_sibling(0, y, c).wait_send()
    for k in range(1, ny):
        to_sibling(k, along(y, -k, ny), c).wait_send()
    for _, up, down, jumps in depths:
        for q in range(share):
            for sub in range(PIECES):
                when_role(q, jumps[2 * sub // PIECES], lambda: z_jump(q, sub).wait_send())
                when_role(q, up, lambda: z_copy(q, sub, 0).wait_send())
                when_role(q, down, lambda: z_copy(q, sub, 1).wait_send())
    for q in range(share):
        for k in range(1, nx):
            ship(q, k, x).wait_send()
            ship(q, k, along(x, -k, nx)).wait_recv()


def local(nx, nz, wave, left, right, left_sizes, right_sizes, charge_left, charge_right, shift):
    block = left.shape[2]
    ny = nx
    half = nz // 2
    share = half // nx
    terms = 2 * ny
    sectors = nx * nz
    entries, _, _ = ring_plan(nz)
    hbm = pl.BlockSpec(memory_space=pl.ANY)
    dma = pltpu.SemaphoreType.DMA
    half_float = jnp.bfloat16
    return pl.pallas_call(
        functools.partial(kernel, nx, nz, block),
        out_shape=jax.ShapeDtypeStruct((block, half * block), jnp.bfloat16),
        in_specs=[hbm] * 8,
        out_specs=pl.BlockSpec(memory_space=pltpu.VMEM),
        scratch_shapes=[
            pltpu.SMEM((sectors,), jnp.int32),
            pltpu.SMEM((sectors,), jnp.int32),
            pltpu.SMEM((sectors,), jnp.int32),
            pltpu.SMEM((sectors,), jnp.int32),
            pltpu.SMEM((1,), jnp.int32),
            dma((5,)),
            pltpu.VMEM((share, terms, block, block), half_float),
            pltpu.VMEM((3, nx, block, share * block), half_float),
            pltpu.VMEM((3, block, block), half_float),
            pltpu.VMEM((2, ny, nx, block + 16, block), half_float),
            pltpu.VMEM((3, nx * block, block), half_float),
            pltpu.VMEM((nx, terms * block, block), half_float),
            pltpu.VMEM((share, nx, block, block), half_float),
            dma((len(entries),)),
            dma((share, terms)),
            dma((share, PIECES, 2)),
            dma((share, PIECES)),
            dma((share, PIECES)),
            dma((3, nx)),
            dma((3, nx)),
            dma((2,)),
            dma((3,)),
            dma((nx - 1,)),
            dma((nx - 1,)),
            dma((ny - 1,)),
            dma((ny - 1,)),
            dma((ny,)),
            dma((ny,)),
            dma((share, nx - 1)),
            dma((share, nx - 1)),
        ],
        compiler_params=pltpu.CompilerParams(
            collective_id=0, has_side_effects=True, vmem_limit_bytes=60 << 20
        ),
        cost_estimate=pl.CostEstimate(
            flops=4 * terms * half * block**3, bytes_accessed=1 << 20, transcendentals=0
        ),
    )(wave, left, right, left_sizes, right_sizes, charge_left, charge_right, shift)


def solution(mesh):
    sectors, terms = mesh.shape["sector"], mesh.shape["term"]
    nx = terms // 2
    placed = (
        P("sector", None),
        P("term", "sector", None, None),
        P("term", "sector", None, None),
        P(),
        P(),
        P(),
        P(),
        P("term"),
    )
    return jax.shard_map(
        functools.partial(local, nx, sectors // nx),
        mesh=mesh,
        in_specs=placed,
        out_specs=P("sector", "term"),
        check_vma=False,
    )
```

```python
import functools

import jax
import jax.numpy as jnp
from jax import lax
from jax.experimental import pallas as pl
from jax.experimental.pallas import tpu as pltpu
from jax.sharding import PartitionSpec as P

MESH = pl.DeviceIdType.MESH
PIECES = 4


def ring_plan(nz):
    entries = (0, 5, 11) if nz == 16 else (0, 3, 7) if nz == 10 else (0,)
    middle = nz // 2
    near = middle - 1

    def comes(offset):
        if offset == middle:
            return nz, 0
        below = min((offset - e) % nz for e in entries)
        above = min((e - offset) % nz for e in entries)
        return (0, 0) if below == 0 else (below, 1) if below < above else (above, -1)

    depths = []
    for depth in sorted({comes(offset)[0] for offset in range(nz)}):
        have = [offset for offset in range(nz) if comes(offset)[0] == depth]
        up = [offset for offset in have if comes((offset + 1) % nz)[1] == 1]
        down = [offset for offset in have if comes((offset - 1) % nz)[1] == -1]
        jump_up = [offset for offset in have if offset == near]
        jump_down = [offset for offset in have if offset == (nz - near) % nz]
        depths.append((have, up, down, (jump_up, jump_down)))
    return entries, middle - near, depths


def one_of(value, choices):
    return functools.reduce(jnp.logical_or, [value == choice for choice in choices])


def kernel(
    nx,
    nz,
    block,
    wave,
    left,
    right,
    left_sizes_in,
    right_sizes_in,
    charge_left_in,
    charge_right_in,
    shift_in,
    out,
    left_sizes,
    right_sizes,
    charge_left,
    charge_right,
    shift,
    scalar_sem,
    rbuf,
    w3,
    l3,
    lbuf,
    mw,
    inner,
    obuf,
    s1_send,
    s1_recv,
    z_send,
    z_recv,
    jump_send,
    w_send,
    w_recv,
    l_send,
    l_recv,
    lx_send,
    lx_recv,
    ly_send,
    ly_recv,
    sib_send,
    sib_recv,
    o_send,
    o_recv,
    own_sem,
):
    ny = nx
    half = nz // 2
    share = half // nx
    sectors = nx * nz
    terms = 2 * ny
    width = half * block
    part_width = share * block
    s = lax.axis_index("sector")
    t = lax.axis_index("term")
    x = s // nz
    z = lax.rem(s, nz)
    y = t // 2
    c = lax.rem(t, 2)
    entries, jump, depths = ring_plan(nz)

    def dev(xx, yy, zz, cc):
        return (xx * nz + zz, yy * 2 + cc)

    def along(value, step, size):
        return lax.rem(value + step + size, size)

    origins = [c * half + x * share + q for q in range(share)]
    roles = [lax.rem(z - origin + nz, nz) for origin in origins]
    above, below = along(z, 1, nz), along(z, -1, nz)
    z_sides = (dev(x, y, above, c), dev(x, y, below, c))
    z_jumps = (dev(x, y, along(z, jump, nz), c), dev(x, y, along(z, -jump, nz), c))
    sibling = (s, t + 1 - 2 * c)
    s_next, s_prev = lax.rem(s + 1, sectors), lax.rem(s + sectors - 1, sectors)

    ring_x, ring_c = lax.rem(z, half) // share, z // half
    mirror = jnp.logical_and(jnp.logical_and(ring_x == x, x == y), ring_c == c)

    def columns(xx):
        start = pl.multiple_of(t * width + xx * part_width, 128)
        return wave.at[:, pl.ds(start, part_width)]

    left_own = left.at[0, 0]
    w_load = pltpu.make_async_copy(columns(x), w3.at[1, x], w_recv.at[1, x])
    l_load = pltpu.make_async_copy(left_own, l3.at[1], l_recv.at[1])
    l_load.start()
    w_load.start()
    scalars = [
        pltpu.make_async_copy(source, held, scalar_sem.at[i])
        for i, (source, held) in enumerate(
            (
                (shift_in, shift),
                (left_sizes_in, left_sizes),
                (right_sizes_in, right_sizes),
                (charge_left_in, charge_left),
                (charge_right_in, charge_right),
            )
        )
    ]
    for copy in scalars:
        copy.start()

    barrier = pltpu.get_barrier_semaphore()

    def greet(target):
        pl.semaphore_signal(barrier, inc=1, device_id=target, device_id_type=MESH)

    for q in range(share):

        @pl.when(one_of(roles[q], entries))
        def _():
            for yy in range(ny):
                for cc in range(2):
                    itself = jnp.logical_and(
                        jnp.logical_and(x == y, z == origins[q]),
                        jnp.logical_and(yy == y, cc == c),
                    )

                    @pl.when(jnp.logical_not(itself))
                    def _():
                        greet(dev(y, yy, origins[q], cc))

    for xx in range(nx):
        greet(dev(xx, y, above, c))
        greet(dev(xx, y, below, c))
    for target in (*z_jumps, sibling):
        greet(target)
    for k in range(1, nx):
        greet(dev(along(x, k, nx), y, z, c))
        greet(dev(x, along(y, k, ny), z, c))
    partners = 2 * nx + 3 + 2 * (nx - 1)
    pl.semaphore_wait(barrier, partners + len(entries) - mirror.astype(jnp.int32))

    def remote(src, dst, send_sem, recv_sem, target):
        return pltpu.make_async_remote_copy(
            src_ref=src,
            dst_ref=dst,
            send_sem=send_sem,
            recv_sem=recv_sem,
            device_id=target,
            device_id_type=MESH,
        )

    l_up = remote(left_own, l3.at[0], l_send.at[0], l_recv.at[0], (s_next, t))
    l_down = remote(left_own, l3.at[2], l_send.at[1], l_recv.at[2], (s_prev, t))
    l_up.start()
    l_down.start()

    right_own = right.at[0, 0]
    own_q = lax.rem(z, share)
    landing, landed = rbuf.at[own_q, t], s1_recv.at[own_q, t]
    first = [
        remote(right_own, landing, s1_send.at[e], landed, dev(ring_x, x, along(z, off, nz), ring_c))
        for e, off in enumerate(entries)
    ]
    for copy in first[1:]:
        copy.start()

    @pl.when(mirror)
    def _():
        pltpu.make_async_copy(right_own, landing, landed).start()

    @pl.when(jnp.logical_not(mirror))
    def _():
        first[0].start()

    waves = []
    for d, row_to in ((0, s_next), (2, s_prev)):
        for xx in range(nx):
            target = dev(xx, y, lax.rem(row_to, nz), c)
            dst = w3.at[d, row_to // nz]
            waves.append(
                remote(columns(xx), dst, w_send.at[d, xx], w_recv.at[d, row_to // nz], target)
            )
    for k in range(1, nx):
        xx = along(x, k, nx)
        waves.append(
            remote(columns(xx), w3.at[1, x], w_send.at[1, k], w_recv.at[1, x], dev(xx, y, z, c))
        )

    scalars[0].wait()
    l_load.wait()
    l_up.wait_recv()
    l_down.wait_recv()
    lbuf[c, y, x, 0:block, :] = l3[1 - shift[0]]
    lbuf[c, y, x, block : block + 16, :] = (
        jnp.full((16, block), shift[0], jnp.int32).astype(jnp.float32).astype(jnp.bfloat16)
    )

    def along_x(k, of):
        part = lbuf.at[c, y, of]
        target = dev(along(x, k, nx), y, z, c)
        return remote(part, part, lx_send.at[k - 1], lx_recv.at[k - 1], target)

    def along_y(k, of):
        part = lbuf.at[c, of]
        target = dev(x, along(y, k, ny), z, c)
        return remote(part, part, ly_send.at[k - 1], ly_recv.at[k - 1], target)

    def to_sibling(k, of, core):
        part = lbuf.at[core, of]
        return remote(part, part, sib_send.at[k], sib_recv.at[k], sibling)

    for k in range(1, nx):
        along_x(k, x).start()
    for copy in waves[: 2 * nx]:
        copy.start()

    blocks = terms // PIECES

    def z_part(q, sub):
        return rbuf.at[q, pl.ds(sub * blocks, blocks)]

    def z_copy(q, sub, side):
        part = z_part(q, sub)
        return remote(part, part, z_send.at[q, sub, side], z_recv.at[q, sub], z_sides[side])

    def z_jump(q, sub):
        part = z_part(q, sub)
        return remote(part, part, jump_send.at[q, sub], z_recv.at[q, sub], z_jumps[2 * sub // PIECES])

    def when_role(q, offsets, act):
        if offsets:
            pl.when(one_of(roles[q], offsets))(act)

    for have, up, down, jumps in depths:
        for q in range(share):

            def pass_on(q=q, have=have, up=up, down=down, jumps=jumps):
                for sub in range(PIECES):
                    if have[0] in entries:
                        for k in range(sub * blocks, (sub + 1) * blocks):
                            copy = remote(
                                right_own, rbuf.at[q, k], s1_send.at[0], s1_recv.at[q, k], sibling
                            )
                            copy.wait_recv()
                    else:
                        z_copy(q, sub, 0).wait_recv()
                    when_role(q, jumps[2 * sub // PIECES], lambda: z_jump(q, sub).start())
                    when_role(q, up, lambda: z_copy(q, sub, 0).start())
                    when_role(q, down, lambda: z_copy(q, sub, 1).start())

            when_role(q, have, pass_on)
        if have is depths[1][0]:
            for copy in waves[2 * nx :]:
                copy.start()
        if have is depths[min(2, len(depths) - 1)][0]:
            for k in range(1, ny):
                of = along(y, -k, ny)
                along_y(k, of).wait_recv()
                to_sibling(k, of, c).start()
        if have[0] in entries:
            for k in range(1, nx):
                along_x(k, along(x, -k, nx)).wait_recv()
            for k in range(1, ny):
                along_y(k, y).start()
            to_sibling(0, y, c).start()

    for copy in scalars[1:]:
        copy.wait()
    w_load.wait()
    for d in range(3):
        for k in range(nx):
            of = along(x, k, nx)
            if d == 1 and k == 0:
                continue
            part = w3.at[d, of]
            remote(part, part, w_send.at[d, 0], w_recv.at[d, of], sibling).wait_recv()
    for k in range(ny):
        to_sibling(k, along(y, -k, ny), 1 - c).wait_recv()

    row = lax.broadcasted_iota(jnp.int32, (block, block), 0)
    col = lax.broadcasted_iota(jnp.int32, (block, block), 1)

    def allowed(a, b):
        inside = jnp.logical_and(a >= 0, a < sectors)
        a = jnp.clip(a, 0, sectors - 1)
        pair = jnp.abs(charge_left[a] - charge_right[b]) <= 1
        rows = jnp.where(inside, left_sizes[a], 0)
        cols = jnp.where(pair, right_sizes[b], 0)
        return jnp.logical_and(row < rows, col < cols)

    def ship(q, k, of):
        xx = along(x, k, nx)
        place = pl.multiple_of(of * part_width + q * block, 128)
        dst = out.at[:, pl.ds(place, block)]
        return remote(
            obuf.at[q, xx], dst, o_send.at[q, k - 1], o_recv.at[q, k - 1], dev(xx, y, z, c)
        )

    def keep_own(q):
        place = pl.multiple_of(x * part_width + q * block, 128)
        return pltpu.make_async_copy(obuf.at[q, x], out.at[:, pl.ds(place, block)], own_sem.at[q])

    @pl.loop(0, share)
    def _(q):
        b = y * nz + c * half + x * share + q
        at = pl.ds(pl.multiple_of(q * block, 128), block)
        for xx in range(nx):
            for d in range(3):
                part = w3[d, xx, :, at].astype(jnp.float32)
                keep = allowed(nz * xx + z + d - 1, b)
                mw[d, xx * block : (xx + 1) * block, :] = jnp.where(keep, part, 0.0).astype(
                    jnp.bfloat16
                )
        for term in range(terms):
            d = lbuf[term % 2, term // 2, 0, block : block + 16, :].astype(jnp.float32)
            rise = (d * (d + 1.0) * 0.5).astype(jnp.bfloat16)
            fall = (d * (d - 1.0) * 0.5).astype(jnp.bfloat16)
            stay = (1.0 - d * d).astype(jnp.bfloat16)
            rise, fall, stay = (
                jnp.concatenate([m] * (nx * block // 16), axis=0) for m in (rise, fall, stay)
            )
            chosen = mw[1] * stay + mw[0] * rise + mw[2] * fall
            product = lax.dot_general(
                chosen, rbuf[q, term], (((1,), (1,)), ((), ())), preferred_element_type=jnp.float32
            ).astype(jnp.bfloat16)
            for xx in range(nx):
                inner[xx, term * block : (term + 1) * block, :] = product[
                    xx * block : (xx + 1) * block
                ]
        for xx in range(nx):
            lefts = jnp.concatenate(
                [lbuf[term % 2, term // 2, xx, 0:block, :] for term in range(terms)], axis=1
            )
            total = jnp.dot(lefts, inner[xx], preferred_element_type=jnp.float32)
            keep = allowed(nz * xx + z, b)
            obuf[q, xx] = jnp.where(keep, total, 0.0).astype(jnp.bfloat16)
        for k in range(1, nx):
            ship(q, k, x).start()
        keep_own(q).start()

    for copy in first[1:]:
        copy.wait_send()

    @pl.when(jnp.logical_not(mirror))
    def _():
        first[0].wait_send()

    for copy in (l_up, l_down, *waves):
        copy.wait_send()
    for k in range(1, nx):
        along_x(k, x).wait_send()
        along_y(k, y).wait_send()
    to_sibling(0, y, c).wait_send()
    for k in range(1, ny):
        to_sibling(k, along(y, -k, ny), c).wait_send()
    for _, up, down, jumps in depths:
        for q in range(share):
            for sub in range(PIECES):
                when_role(q, jumps[2 * sub // PIECES], lambda: z_jump(q, sub).wait_send())
                when_role(q, up, lambda: z_copy(q, sub, 0).wait_send())
                when_role(q, down, lambda: z_copy(q, sub, 1).wait_send())
    for q in range(share):
        keep_own(q).wait()
        for k in range(1, nx):
            ship(q, k, x).wait_send()
            ship(q, k, along(x, -k, nx)).wait_recv()


def local(nx, nz, wave, left, right, left_sizes, right_sizes, charge_left, charge_right, shift):
    block = left.shape[2]
    ny = nx
    half = nz // 2
    share = half // nx
    terms = 2 * ny
    sectors = nx * nz
    entries, _, _ = ring_plan(nz)
    hbm = pl.BlockSpec(memory_space=pl.ANY)
    dma = pltpu.SemaphoreType.DMA
    half_float = jnp.bfloat16
    return pl.pallas_call(
        functools.partial(kernel, nx, nz, block),
        out_shape=jax.ShapeDtypeStruct((block, half * block), jnp.bfloat16),
        in_specs=[hbm] * 8,
        out_specs=pl.BlockSpec(memory_space=pl.ANY),
        scratch_shapes=[
            pltpu.SMEM((sectors,), jnp.int32),
            pltpu.SMEM((sectors,), jnp.int32),
            pltpu.SMEM((sectors,), jnp.int32),
            pltpu.SMEM((sectors,), jnp.int32),
            pltpu.SMEM((1,), jnp.int32),
            dma((5,)),
            pltpu.VMEM((share, terms, block, block), half_float),
            pltpu.VMEM((3, nx, block, share * block), half_float),
            pltpu.VMEM((3, block, block), half_float),
            pltpu.VMEM((2, ny, nx, block + 16, block), half_float),
            pltpu.VMEM((3, nx * block, block), half_float),
            pltpu.VMEM((nx, terms * block, block), half_float),
            pltpu.VMEM((share, nx, block, block), half_float),
            dma((len(entries),)),
            dma((share, terms)),
            dma((share, PIECES, 2)),
            dma((share, PIECES)),
            dma((share, PIECES)),
            dma((3, nx)),
            dma((3, nx)),
            dma((2,)),
            dma((3,)),
            dma((nx - 1,)),
            dma((nx - 1,)),
            dma((ny - 1,)),
            dma((ny - 1,)),
            dma((ny,)),
            dma((ny,)),
            dma((share, nx - 1)),
            dma((share, nx - 1)),
            dma((share,)),
        ],
        compiler_params=pltpu.CompilerParams(
            collective_id=0, has_side_effects=True, vmem_limit_bytes=60 << 20
        ),
        cost_estimate=pl.CostEstimate(
            flops=4 * terms * half * block**3, bytes_accessed=1 << 20, transcendentals=0
        ),
    )(wave, left, right, left_sizes, right_sizes, charge_left, charge_right, shift)


def solution(mesh):
    sectors, terms = mesh.shape["sector"], mesh.shape["term"]
    nx = terms // 2
    placed = (
        P("sector", None),
        P("term", "sector", None, None),
        P("term", "sector", None, None),
        P(),
        P(),
        P(),
        P(),
        P("term"),
    )
    return jax.shard_map(
        functools.partial(local, nx, sectors // nx),
        mesh=mesh,
        in_specs=placed,
        out_specs=P("sector", "term"),
        check_vma=False,
    )
```

```python
import functools

import jax
import jax.numpy as jnp
from jax import lax
from jax.experimental import pallas as pl
from jax.experimental.pallas import tpu as pltpu
from jax.sharding import PartitionSpec as P

MESH = pl.DeviceIdType.MESH
PIECES = 4


def ring_plan(nz):
    entries = (0, 5, 11) if nz == 16 else (0, 3, 7) if nz == 10 else (0,)
    middle = nz // 2
    near = middle - 1

    def comes(offset):
        if offset == middle:
            return nz, 0
        below = min((offset - e) % nz for e in entries)
        above = min((e - offset) % nz for e in entries)
        return (0, 0) if below == 0 else (below, 1) if below < above else (above, -1)

    depths = []
    for depth in sorted({comes(offset)[0] for offset in range(nz)}):
        have = [offset for offset in range(nz) if comes(offset)[0] == depth]
        up = [offset for offset in have if comes((offset + 1) % nz)[1] == 1]
        down = [offset for offset in have if comes((offset - 1) % nz)[1] == -1]
        jump_up = [offset for offset in have if offset == near]
        jump_down = [offset for offset in have if offset == (nz - near) % nz]
        depths.append((have, up, down, (jump_up, jump_down)))
    return entries, middle - near, depths


def one_of(value, choices):
    return functools.reduce(jnp.logical_or, [value == choice for choice in choices])


def kernel(
    nx,
    nz,
    block,
    wave,
    left,
    right,
    left_sizes_in,
    right_sizes_in,
    charge_left_in,
    charge_right_in,
    shift_in,
    out,
    left_sizes,
    right_sizes,
    charge_left,
    charge_right,
    shift,
    scalar_sem,
    rbuf,
    w3,
    l3,
    lbuf,
    mw,
    inner,
    obuf,
    s1_send,
    s1_recv,
    z_send,
    z_recv,
    jump_send,
    w_send,
    w_recv,
    l_send,
    l_recv,
    lx_send,
    lx_recv,
    ly_send,
    ly_recv,
    sib_send,
    sib_recv,
    o_send,
    o_recv,
    own_sem,
):
    ny = nx
    half = nz // 2
    share = half // nx
    sectors = nx * nz
    terms = 2 * ny
    width = half * block
    part_width = share * block
    s = lax.axis_index("sector")
    t = lax.axis_index("term")
    x = s // nz
    z = lax.rem(s, nz)
    y = t // 2
    c = lax.rem(t, 2)
    entries, jump, depths = ring_plan(nz)

    def dev(xx, yy, zz, cc):
        return (xx * nz + zz, yy * 2 + cc)

    def along(value, step, size):
        return lax.rem(value + step + size, size)

    origins = [c * half + x * share + q for q in range(share)]
    roles = [lax.rem(z - origin + nz, nz) for origin in origins]
    above, below = along(z, 1, nz), along(z, -1, nz)
    z_sides = (dev(x, y, above, c), dev(x, y, below, c))
    z_jumps = (dev(x, y, along(z, jump, nz), c), dev(x, y, along(z, -jump, nz), c))
    sibling = (s, t + 1 - 2 * c)
    s_next, s_prev = lax.rem(s + 1, sectors), lax.rem(s + sectors - 1, sectors)

    ring_x, ring_c = lax.rem(z, half) // share, z // half
    mirror = jnp.logical_and(jnp.logical_and(ring_x == x, x == y), ring_c == c)

    def columns(xx):
        start = pl.multiple_of(t * width + xx * part_width, 128)
        return wave.at[:, pl.ds(start, part_width)]

    left_own = left.at[0, 0]
    w_load = pltpu.make_async_copy(columns(x), w3.at[1, x], w_recv.at[1, x])
    l_load = pltpu.make_async_copy(left_own, l3.at[1], l_recv.at[1])
    l_load.start()
    w_load.start()
    scalars = [
        pltpu.make_async_copy(source, held, scalar_sem.at[i])
        for i, (source, held) in enumerate(
            (
                (shift_in, shift),
                (left_sizes_in, left_sizes),
                (right_sizes_in, right_sizes),
                (charge_left_in, charge_left),
                (charge_right_in, charge_right),
            )
        )
    ]
    for copy in scalars:
        copy.start()

    barrier = pltpu.get_barrier_semaphore()

    def greet(target):
        pl.semaphore_signal(barrier, inc=1, device_id=target, device_id_type=MESH)

    for q in range(share):

        @pl.when(one_of(roles[q], entries))
        def _():
            for yy in range(ny):
                for cc in range(2):
                    itself = jnp.logical_and(
                        jnp.logical_and(x == y, z == origins[q]),
                        jnp.logical_and(yy == y, cc == c),
                    )

                    @pl.when(jnp.logical_not(itself))
                    def _():
                        greet(dev(y, yy, origins[q], cc))

    for xx in range(nx):
        greet(dev(xx, y, above, c))
        greet(dev(xx, y, below, c))
    for target in (*z_jumps, sibling):
        greet(target)
    for k in range(1, nx):
        greet(dev(along(x, k, nx), y, z, c))
        greet(dev(x, along(y, k, ny), z, c))
    partners = 2 * nx + 3 + 2 * (nx - 1)
    pl.semaphore_wait(barrier, partners + len(entries) - mirror.astype(jnp.int32))

    def remote(src, dst, send_sem, recv_sem, target):
        return pltpu.make_async_remote_copy(
            src_ref=src,
            dst_ref=dst,
            send_sem=send_sem,
            recv_sem=recv_sem,
            device_id=target,
            device_id_type=MESH,
        )

    l_up = remote(left_own, l3.at[0], l_send.at[0], l_recv.at[0], (s_next, t))
    l_down = remote(left_own, l3.at[2], l_send.at[1], l_recv.at[2], (s_prev, t))
    l_up.start()
    l_down.start()

    right_own = right.at[0, 0]
    own_q = lax.rem(z, share)
    landing, landed = rbuf.at[own_q, t], s1_recv.at[own_q, t]
    first = [
        remote(right_own, landing, s1_send.at[e], landed, dev(ring_x, x, along(z, off, nz), ring_c))
        for e, off in enumerate(entries)
    ]
    for copy in first[1:]:
        copy.start()

    @pl.when(mirror)
    def _():
        pltpu.make_async_copy(right_own, landing, landed).start()

    @pl.when(jnp.logical_not(mirror))
    def _():
        first[0].start()

    waves = []
    for d, row_to in ((0, s_next), (2, s_prev)):
        for xx in range(nx):
            target = dev(xx, y, lax.rem(row_to, nz), c)
            dst = w3.at[d, row_to // nz]
            waves.append(
                remote(columns(xx), dst, w_send.at[d, xx], w_recv.at[d, row_to // nz], target)
            )
    for k in range(1, nx):
        xx = along(x, k, nx)
        waves.append(
            remote(columns(xx), w3.at[1, x], w_send.at[1, k], w_recv.at[1, x], dev(xx, y, z, c))
        )

    scalars[0].wait()
    l_load.wait()
    l_up.wait_recv()
    l_down.wait_recv()
    lbuf[c, y, x, 0:block, :] = l3[1 - shift[0]]
    lbuf[c, y, x, block : block + 16, :] = (
        jnp.full((16, block), shift[0], jnp.int32).astype(jnp.float32).astype(jnp.bfloat16)
    )

    def along_x(k, of):
        part = lbuf.at[c, y, of]
        target = dev(along(x, k, nx), y, z, c)
        return remote(part, part, lx_send.at[k - 1], lx_recv.at[k - 1], target)

    def along_y(k, of):
        part = lbuf.at[c, of]
        target = dev(x, along(y, k, ny), z, c)
        return remote(part, part, ly_send.at[k - 1], ly_recv.at[k - 1], target)

    def to_sibling(k, of, core):
        part = lbuf.at[core, of]
        return remote(part, part, sib_send.at[k], sib_recv.at[k], sibling)

    for k in range(1, nx):
        along_x(k, x).start()
    for copy in waves[: 2 * nx]:
        copy.start()

    blocks = terms // PIECES

    def z_part(q, sub):
        return rbuf.at[q, pl.ds(sub * blocks, blocks)]

    def z_copy(q, sub, side):
        part = z_part(q, sub)
        return remote(part, part, z_send.at[q, sub, side], z_recv.at[q, sub], z_sides[side])

    def z_jump(q, sub):
        part = z_part(q, sub)
        return remote(part, part, jump_send.at[q, sub], z_recv.at[q, sub], z_jumps[2 * sub // PIECES])

    def when_role(q, offsets, act):
        if offsets:
            pl.when(one_of(roles[q], offsets))(act)

    for have, up, down, jumps in depths:
        for q in range(share):

            def pass_on(q=q, have=have, up=up, down=down, jumps=jumps):
                for sub in range(PIECES):
                    if have[0] in entries:
                        for k in range(sub * blocks, (sub + 1) * blocks):
                            copy = remote(
                                right_own, rbuf.at[q, k], s1_send.at[0], s1_recv.at[q, k], sibling
                            )
                            copy.wait_recv()
                    else:
                        z_copy(q, sub, 0).wait_recv()
                    when_role(q, jumps[2 * sub // PIECES], lambda: z_jump(q, sub).start())
                    when_role(q, up, lambda: z_copy(q, sub, 0).start())
                    when_role(q, down, lambda: z_copy(q, sub, 1).start())

            when_role(q, have, pass_on)
        if have is depths[1][0]:
            for copy in waves[2 * nx :]:
                copy.start()
        if have is depths[min(2, len(depths) - 1)][0]:
            for k in range(1, ny):
                of = along(y, -k, ny)
                along_y(k, of).wait_recv()
                to_sibling(k, of, c).start()
        if have[0] in entries:
            for k in range(1, nx):
                along_x(k, along(x, -k, nx)).wait_recv()
            for k in range(1, ny):
                along_y(k, y).start()
            to_sibling(0, y, c).start()

    for copy in scalars[1:]:
        copy.wait()
    w_load.wait()
    for d in range(3):
        for k in range(nx):
            of = along(x, k, nx)
            if d == 1 and k == 0:
                continue
            part = w3.at[d, of]
            remote(part, part, w_send.at[d, 0], w_recv.at[d, of], sibling).wait_recv()
    for k in range(ny):
        to_sibling(k, along(y, -k, ny), 1 - c).wait_recv()

    row = lax.broadcasted_iota(jnp.int32, (block, block), 0)
    col = lax.broadcasted_iota(jnp.int32, (block, block), 1)

    def allowed(a, b):
        inside = jnp.logical_and(a >= 0, a < sectors)
        a = jnp.clip(a, 0, sectors - 1)
        pair = jnp.abs(charge_left[a] - charge_right[b]) <= 1
        rows = jnp.where(inside, left_sizes[a], 0)
        cols = jnp.where(pair, right_sizes[b], 0)
        return jnp.logical_and(row < rows, col < cols)

    def ship(q, k, of):
        xx = along(x, k, nx)
        place = pl.multiple_of(of * part_width + q * block, 128)
        dst = out.at[:, pl.ds(place, block)]
        return remote(
            obuf.at[q, xx], dst, o_send.at[q, k - 1], o_recv.at[q, k - 1], dev(xx, y, z, c)
        )

    def keep_own(q):
        place = pl.multiple_of(x * part_width + q * block, 128)
        return pltpu.make_async_copy(obuf.at[q, x], out.at[:, pl.ds(place, block)], own_sem.at[q])

    @pl.loop(0, share)
    def _(q):
        b = y * nz + c * half + x * share + q
        at = pl.ds(pl.multiple_of(q * block, 128), block)
        for xx in range(nx):
            for d in range(3):
                part = w3[d, xx, :, at].astype(jnp.float32)
                keep = allowed(nz * xx + z + d - 1, b)
                mw[d, xx * block : (xx + 1) * block, :] = jnp.where(keep, part, 0.0).astype(
                    jnp.bfloat16
                )
        for term in range(terms):
            d = lbuf[term % 2, term // 2, 0, block : block + 16, :].astype(jnp.float32)
            rise = (d * (d + 1.0) * 0.5).astype(jnp.bfloat16)
            fall = (d * (d - 1.0) * 0.5).astype(jnp.bfloat16)
            stay = (1.0 - d * d).astype(jnp.bfloat16)
            rise, fall, stay = (
                jnp.concatenate([m] * (nx * block // 16), axis=0) for m in (rise, fall, stay)
            )
            chosen = mw[1] * stay + mw[0] * rise + mw[2] * fall
            product = lax.dot_general(
                chosen, rbuf[q, term], (((1,), (1,)), ((), ())), preferred_element_type=jnp.float32
            ).astype(jnp.bfloat16)
            for xx in range(nx):
                inner[xx, term * block : (term + 1) * block, :] = product[
                    xx * block : (xx + 1) * block
                ]
        for xx in range(nx):
            lefts = jnp.concatenate(
                [lbuf[term % 2, term // 2, xx, 0:block, :] for term in range(terms)], axis=1
            )
            total = jnp.dot(lefts, inner[xx], preferred_element_type=jnp.float32)
            keep = allowed(nz * xx + z, b)
            obuf[q, xx] = jnp.where(keep, total, 0.0).astype(jnp.bfloat16)
        for k in sorted(range(1, nx), key=lambda k: -min(k, nx - k)):
            ship(q, k, x).start()
        keep_own(q).start()

    for copy in first[1:]:
        copy.wait_send()

    @pl.when(jnp.logical_not(mirror))
    def _():
        first[0].wait_send()

    for copy in (l_up, l_down, *waves):
        copy.wait_send()
    for k in range(1, nx):
        along_x(k, x).wait_send()
        along_y(k, y).wait_send()
    to_sibling(0, y, c).wait_send()
    for k in range(1, ny):
        to_sibling(k, along(y, -k, ny), c).wait_send()
    for _, up, down, jumps in depths:
        for q in range(share):
            for sub in range(PIECES):
                when_role(q, jumps[2 * sub // PIECES], lambda: z_jump(q, sub).wait_send())
                when_role(q, up, lambda: z_copy(q, sub, 0).wait_send())
                when_role(q, down, lambda: z_copy(q, sub, 1).wait_send())
    for q in range(share):
        keep_own(q).wait()
        for k in range(1, nx):
            ship(q, k, x).wait_send()
            ship(q, k, along(x, -k, nx)).wait_recv()


def local(nx, nz, wave, left, right, left_sizes, right_sizes, charge_left, charge_right, shift):
    block = left.shape[2]
    ny = nx
    half = nz // 2
    share = half // nx
    terms = 2 * ny
    sectors = nx * nz
    entries, _, _ = ring_plan(nz)
    hbm = pl.BlockSpec(memory_space=pl.ANY)
    dma = pltpu.SemaphoreType.DMA
    half_float = jnp.bfloat16
    return pl.pallas_call(
        functools.partial(kernel, nx, nz, block),
        out_shape=jax.ShapeDtypeStruct((block, half * block), jnp.bfloat16),
        in_specs=[hbm] * 8,
        out_specs=pl.BlockSpec(memory_space=pl.ANY),
        scratch_shapes=[
            pltpu.SMEM((sectors,), jnp.int32),
            pltpu.SMEM((sectors,), jnp.int32),
            pltpu.SMEM((sectors,), jnp.int32),
            pltpu.SMEM((sectors,), jnp.int32),
            pltpu.SMEM((1,), jnp.int32),
            dma((5,)),
            pltpu.VMEM((share, terms, block, block), half_float),
            pltpu.VMEM((3, nx, block, share * block), half_float),
            pltpu.VMEM((3, block, block), half_float),
            pltpu.VMEM((2, ny, nx, block + 16, block), half_float),
            pltpu.VMEM((3, nx * block, block), half_float),
            pltpu.VMEM((nx, terms * block, block), half_float),
            pltpu.VMEM((share, nx, block, block), half_float),
            dma((len(entries),)),
            dma((share, terms)),
            dma((share, PIECES, 2)),
            dma((share, PIECES)),
            dma((share, PIECES)),
            dma((3, nx)),
            dma((3, nx)),
            dma((2,)),
            dma((3,)),
            dma((nx - 1,)),
            dma((nx - 1,)),
            dma((ny - 1,)),
            dma((ny - 1,)),
            dma((ny,)),
            dma((ny,)),
            dma((share, nx - 1)),
            dma((share, nx - 1)),
            dma((share,)),
        ],
        compiler_params=pltpu.CompilerParams(
            collective_id=0, has_side_effects=True, vmem_limit_bytes=60 << 20
        ),
        cost_estimate=pl.CostEstimate(
            flops=4 * terms * half * block**3, bytes_accessed=1 << 20, transcendentals=0
        ),
    )(wave, left, right, left_sizes, right_sizes, charge_left, charge_right, shift)


def solution(mesh):
    sectors, terms = mesh.shape["sector"], mesh.shape["term"]
    nx = terms // 2
    placed = (
        P("sector", None),
        P("term", "sector", None, None),
        P("term", "sector", None, None),
        P(),
        P(),
        P(),
        P(),
        P("term"),
    )
    return jax.shard_map(
        functools.partial(local, nx, sectors // nx),
        mesh=mesh,
        in_specs=placed,
        out_specs=P("sector", "term"),
        check_vma=False,
    )
```

```python
import functools

import jax
import jax.numpy as jnp
from jax import lax
from jax.experimental import pallas as pl
from jax.experimental.pallas import tpu as pltpu
from jax.sharding import PartitionSpec as P

MESH = pl.DeviceIdType.MESH
PIECES = 8


def ring_plan(nz):
    entries = (0, 5, 11) if nz == 16 else (0, 3, 7) if nz == 10 else (0,)
    middle = nz // 2
    near = middle - 1

    def comes(offset):
        if offset == middle:
            return nz, 0
        below = min((offset - e) % nz for e in entries)
        above = min((e - offset) % nz for e in entries)
        return (0, 0) if below == 0 else (below, 1) if below < above else (above, -1)

    depths = []
    for depth in sorted({comes(offset)[0] for offset in range(nz)}):
        have = [offset for offset in range(nz) if comes(offset)[0] == depth]
        up = [offset for offset in have if comes((offset + 1) % nz)[1] == 1]
        down = [offset for offset in have if comes((offset - 1) % nz)[1] == -1]
        jump_up = [offset for offset in have if offset == near]
        jump_down = [offset for offset in have if offset == (nz - near) % nz]
        depths.append((have, up, down, (jump_up, jump_down)))
    return entries, middle - near, depths


def one_of(value, choices):
    return functools.reduce(jnp.logical_or, [value == choice for choice in choices])


def kernel(
    nx,
    nz,
    block,
    wave,
    left,
    right,
    left_sizes_in,
    right_sizes_in,
    charge_left_in,
    charge_right_in,
    shift_in,
    out,
    left_sizes,
    right_sizes,
    charge_left,
    charge_right,
    shift,
    scalar_sem,
    rbuf,
    w3,
    l3,
    lbuf,
    mw,
    inner,
    obuf,
    s1_send,
    s1_recv,
    z_send,
    z_recv,
    jump_send,
    w_send,
    w_recv,
    l_send,
    l_recv,
    lx_send,
    lx_recv,
    ly_send,
    ly_recv,
    sib_send,
    sib_recv,
    o_send,
    o_recv,
    own_sem,
):
    ny = nx
    half = nz // 2
    share = half // nx
    sectors = nx * nz
    terms = 2 * ny
    width = half * block
    part_width = share * block
    s = lax.axis_index("sector")
    t = lax.axis_index("term")
    x = s // nz
    z = lax.rem(s, nz)
    y = t // 2
    c = lax.rem(t, 2)
    entries, jump, depths = ring_plan(nz)

    def dev(xx, yy, zz, cc):
        return (xx * nz + zz, yy * 2 + cc)

    def along(value, step, size):
        return lax.rem(value + step + size, size)

    origins = [c * half + x * share + q for q in range(share)]
    roles = [lax.rem(z - origin + nz, nz) for origin in origins]
    above, below = along(z, 1, nz), along(z, -1, nz)
    z_sides = (dev(x, y, above, c), dev(x, y, below, c))
    z_jumps = (dev(x, y, along(z, jump, nz), c), dev(x, y, along(z, -jump, nz), c))
    sibling = (s, t + 1 - 2 * c)
    s_next, s_prev = lax.rem(s + 1, sectors), lax.rem(s + sectors - 1, sectors)

    ring_x, ring_c = lax.rem(z, half) // share, z // half
    mirror = jnp.logical_and(jnp.logical_and(ring_x == x, x == y), ring_c == c)

    def columns(xx):
        start = pl.multiple_of(t * width + xx * part_width, 128)
        return wave.at[:, pl.ds(start, part_width)]

    left_own = left.at[0, 0]
    w_load = pltpu.make_async_copy(columns(x), w3.at[1, x], w_recv.at[1, x])
    l_load = pltpu.make_async_copy(left_own, l3.at[1], l_recv.at[1])
    l_load.start()
    w_load.start()
    scalars = [
        pltpu.make_async_copy(source, held, scalar_sem.at[i])
        for i, (source, held) in enumerate(
            (
                (shift_in, shift),
                (left_sizes_in, left_sizes),
                (right_sizes_in, right_sizes),
                (charge_left_in, charge_left),
                (charge_right_in, charge_right),
            )
        )
    ]
    for copy in scalars:
        copy.start()

    barrier = pltpu.get_barrier_semaphore()

    def greet(target):
        pl.semaphore_signal(barrier, inc=1, device_id=target, device_id_type=MESH)

    for q in range(share):

        @pl.when(one_of(roles[q], entries))
        def _():
            for yy in range(ny):
                for cc in range(2):
                    itself = jnp.logical_and(
                        jnp.logical_and(x == y, z == origins[q]),
                        jnp.logical_and(yy == y, cc == c),
                    )

                    @pl.when(jnp.logical_not(itself))
                    def _():
                        greet(dev(y, yy, origins[q], cc))

    for xx in range(nx):
        greet(dev(xx, y, above, c))
        greet(dev(xx, y, below, c))
    for target in (*z_jumps, sibling):
        greet(target)
    for k in range(1, nx):
        greet(dev(along(x, k, nx), y, z, c))
        greet(dev(x, along(y, k, ny), z, c))
    partners = 2 * nx + 3 + 2 * (nx - 1)
    pl.semaphore_wait(barrier, partners + len(entries) - mirror.astype(jnp.int32))

    def remote(src, dst, send_sem, recv_sem, target):
        return pltpu.make_async_remote_copy(
            src_ref=src,
            dst_ref=dst,
            send_sem=send_sem,
            recv_sem=recv_sem,
            device_id=target,
            device_id_type=MESH,
        )

    l_up = remote(left_own, l3.at[0], l_send.at[0], l_recv.at[0], (s_next, t))
    l_down = remote(left_own, l3.at[2], l_send.at[1], l_recv.at[2], (s_prev, t))
    l_up.start()
    l_down.start()

    right_own = right.at[0, 0]
    own_q = lax.rem(z, share)
    landing, landed = rbuf.at[own_q, t], s1_recv.at[own_q, t]
    first = [
        remote(right_own, landing, s1_send.at[e], landed, dev(ring_x, x, along(z, off, nz), ring_c))
        for e, off in enumerate(entries)
    ]
    for copy in first[1:]:
        copy.start()

    @pl.when(mirror)
    def _():
        pltpu.make_async_copy(right_own, landing, landed).start()

    @pl.when(jnp.logical_not(mirror))
    def _():
        first[0].start()

    waves = []
    for d, row_to in ((0, s_next), (2, s_prev)):
        for xx in range(nx):
            target = dev(xx, y, lax.rem(row_to, nz), c)
            dst = w3.at[d, row_to // nz]
            waves.append(
                remote(columns(xx), dst, w_send.at[d, xx], w_recv.at[d, row_to // nz], target)
            )
    for k in range(1, nx):
        xx = along(x, k, nx)
        waves.append(
            remote(columns(xx), w3.at[1, x], w_send.at[1, k], w_recv.at[1, x], dev(xx, y, z, c))
        )

    scalars[0].wait()
    l_load.wait()
    l_up.wait_recv()
    l_down.wait_recv()
    lbuf[c, y, x, 0:block, :] = l3[1 - shift[0]]
    lbuf[c, y, x, block : block + 16, :] = (
        jnp.full((16, block), shift[0], jnp.int32).astype(jnp.float32).astype(jnp.bfloat16)
    )

    def along_x(k, of):
        part = lbuf.at[c, y, of]
        target = dev(along(x, k, nx), y, z, c)
        return remote(part, part, lx_send.at[k - 1], lx_recv.at[k - 1], target)

    def along_y(k, of):
        part = lbuf.at[c, of]
        target = dev(x, along(y, k, ny), z, c)
        return remote(part, part, ly_send.at[k - 1], ly_recv.at[k - 1], target)

    def to_sibling(k, of, core):
        part = lbuf.at[core, of]
        return remote(part, part, sib_send.at[k], sib_recv.at[k], sibling)

    for k in range(1, nx):
        along_x(k, x).start()
    for copy in waves[: 2 * nx]:
        copy.start()

    blocks = terms // PIECES

    def z_part(q, sub):
        return rbuf.at[q, pl.ds(sub * blocks, blocks)]

    def z_copy(q, sub, side):
        part = z_part(q, sub)
        return remote(part, part, z_send.at[q, sub, side], z_recv.at[q, sub], z_sides[side])

    def z_jump(q, sub):
        part = z_part(q, sub)
        return remote(part, part, jump_send.at[q, sub], z_recv.at[q, sub], z_jumps[2 * sub // PIECES])

    def when_role(q, offsets, act):
        if offsets:
            pl.when(one_of(roles[q], offsets))(act)

    for have, up, down, jumps in depths:
        for q in range(share):

            def pass_on(q=q, have=have, up=up, down=down, jumps=jumps):
                for sub in range(PIECES):
                    if have[0] in entries:
                        for k in range(sub * blocks, (sub + 1) * blocks):
                            copy = remote(
                                right_own, rbuf.at[q, k], s1_send.at[0], s1_recv.at[q, k], sibling
                            )
                            copy.wait_recv()
                    else:
                        z_copy(q, sub, 0).wait_recv()
                    when_role(q, jumps[2 * sub // PIECES], lambda: z_jump(q, sub).start())
                    when_role(q, up, lambda: z_copy(q, sub, 0).start())
                    when_role(q, down, lambda: z_copy(q, sub, 1).start())

            when_role(q, have, pass_on)
        if have is depths[1][0]:
            for copy in waves[2 * nx :]:
                copy.start()
        if have is depths[min(2, len(depths) - 1)][0]:
            for k in range(1, ny):
                of = along(y, -k, ny)
                along_y(k, of).wait_recv()
                to_sibling(k, of, c).start()
        if have[0] in entries:
            for k in range(1, nx):
                along_x(k, along(x, -k, nx)).wait_recv()
            for k in range(1, ny):
                along_y(k, y).start()
            to_sibling(0, y, c).start()

    for copy in scalars[1:]:
        copy.wait()
    w_load.wait()
    for d in range(3):
        for k in range(nx):
            of = along(x, k, nx)
            if d == 1 and k == 0:
                continue
            part = w3.at[d, of]
            remote(part, part, w_send.at[d, 0], w_recv.at[d, of], sibling).wait_recv()
    for k in range(ny):
        to_sibling(k, along(y, -k, ny), 1 - c).wait_recv()

    row = lax.broadcasted_iota(jnp.int32, (block, block), 0)
    col = lax.broadcasted_iota(jnp.int32, (block, block), 1)

    def allowed(a, b):
        inside = jnp.logical_and(a >= 0, a < sectors)
        a = jnp.clip(a, 0, sectors - 1)
        pair = jnp.abs(charge_left[a] - charge_right[b]) <= 1
        rows = jnp.where(inside, left_sizes[a], 0)
        cols = jnp.where(pair, right_sizes[b], 0)
        return jnp.logical_and(row < rows, col < cols)

    def ship(q, k, of):
        xx = along(x, k, nx)
        place = pl.multiple_of(of * part_width + q * block, 128)
        dst = out.at[:, pl.ds(place, block)]
        return remote(
            obuf.at[q, xx], dst, o_send.at[q, k - 1], o_recv.at[q, k - 1], dev(xx, y, z, c)
        )

    def keep_own(q):
        place = pl.multiple_of(x * part_width + q * block, 128)
        return pltpu.make_async_copy(obuf.at[q, x], out.at[:, pl.ds(place, block)], own_sem.at[q])

    @pl.loop(0, share)
    def _(q):
        b = y * nz + c * half + x * share + q
        at = pl.ds(pl.multiple_of(q * block, 128), block)
        for xx in range(nx):
            for d in range(3):
                part = w3[d, xx, :, at].astype(jnp.float32)
                keep = allowed(nz * xx + z + d - 1, b)
                mw[d, xx * block : (xx + 1) * block, :] = jnp.where(keep, part, 0.0).astype(
                    jnp.bfloat16
                )
        for term in range(terms):
            d = lbuf[term % 2, term // 2, 0, block : block + 16, :].astype(jnp.float32)
            rise = (d * (d + 1.0) * 0.5).astype(jnp.bfloat16)
            fall = (d * (d - 1.0) * 0.5).astype(jnp.bfloat16)
            stay = (1.0 - d * d).astype(jnp.bfloat16)
            rise, fall, stay = (
                jnp.concatenate([m] * (nx * block // 16), axis=0) for m in (rise, fall, stay)
            )
            chosen = mw[1] * stay + mw[0] * rise + mw[2] * fall
            product = lax.dot_general(
                chosen, rbuf[q, term], (((1,), (1,)), ((), ())), preferred_element_type=jnp.float32
            ).astype(jnp.bfloat16)
            for xx in range(nx):
                inner[xx, term * block : (term + 1) * block, :] = product[
                    xx * block : (xx + 1) * block
                ]
        for xx in range(nx):
            lefts = jnp.concatenate(
                [lbuf[term % 2, term // 2, xx, 0:block, :] for term in range(terms)], axis=1
            )
            total = jnp.dot(lefts, inner[xx], preferred_element_type=jnp.float32)
            keep = allowed(nz * xx + z, b)
            obuf[q, xx] = jnp.where(keep, total, 0.0).astype(jnp.bfloat16)
        for k in range(1, nx):
            ship(q, k, x).start()
        keep_own(q).start()

    for copy in first[1:]:
        copy.wait_send()

    @pl.when(jnp.logical_not(mirror))
    def _():
        first[0].wait_send()

    for copy in (l_up, l_down, *waves):
        copy.wait_send()
    for k in range(1, nx):
        along_x(k, x).wait_send()
        along_y(k, y).wait_send()
    to_sibling(0, y, c).wait_send()
    for k in range(1, ny):
        to_sibling(k, along(y, -k, ny), c).wait_send()
    for _, up, down, jumps in depths:
        for q in range(share):
            for sub in range(PIECES):
                when_role(q, jumps[2 * sub // PIECES], lambda: z_jump(q, sub).wait_send())
                when_role(q, up, lambda: z_copy(q, sub, 0).wait_send())
                when_role(q, down, lambda: z_copy(q, sub, 1).wait_send())
    for q in range(share):
        keep_own(q).wait()
        for k in range(1, nx):
            ship(q, k, x).wait_send()
            ship(q, k, along(x, -k, nx)).wait_recv()


def local(nx, nz, wave, left, right, left_sizes, right_sizes, charge_left, charge_right, shift):
    block = left.shape[2]
    ny = nx
    half = nz // 2
    share = half // nx
    terms = 2 * ny
    sectors = nx * nz
    entries, _, _ = ring_plan(nz)
    hbm = pl.BlockSpec(memory_space=pl.ANY)
    dma = pltpu.SemaphoreType.DMA
    half_float = jnp.bfloat16
    return pl.pallas_call(
        functools.partial(kernel, nx, nz, block),
        out_shape=jax.ShapeDtypeStruct((block, half * block), jnp.bfloat16),
        in_specs=[hbm] * 8,
        out_specs=pl.BlockSpec(memory_space=pl.ANY),
        scratch_shapes=[
            pltpu.SMEM((sectors,), jnp.int32),
            pltpu.SMEM((sectors,), jnp.int32),
            pltpu.SMEM((sectors,), jnp.int32),
            pltpu.SMEM((sectors,), jnp.int32),
            pltpu.SMEM((1,), jnp.int32),
            dma((5,)),
            pltpu.VMEM((share, terms, block, block), half_float),
            pltpu.VMEM((3, nx, block, share * block), half_float),
            pltpu.VMEM((3, block, block), half_float),
            pltpu.VMEM((2, ny, nx, block + 16, block), half_float),
            pltpu.VMEM((3, nx * block, block), half_float),
            pltpu.VMEM((nx, terms * block, block), half_float),
            pltpu.VMEM((share, nx, block, block), half_float),
            dma((len(entries),)),
            dma((share, terms)),
            dma((share, PIECES, 2)),
            dma((share, PIECES)),
            dma((share, PIECES)),
            dma((3, nx)),
            dma((3, nx)),
            dma((2,)),
            dma((3,)),
            dma((nx - 1,)),
            dma((nx - 1,)),
            dma((ny - 1,)),
            dma((ny - 1,)),
            dma((ny,)),
            dma((ny,)),
            dma((share, nx - 1)),
            dma((share, nx - 1)),
            dma((share,)),
        ],
        compiler_params=pltpu.CompilerParams(
            collective_id=0, has_side_effects=True, vmem_limit_bytes=60 << 20
        ),
        cost_estimate=pl.CostEstimate(
            flops=4 * terms * half * block**3, bytes_accessed=1 << 20, transcendentals=0
        ),
    )(wave, left, right, left_sizes, right_sizes, charge_left, charge_right, shift)


def solution(mesh):
    sectors, terms = mesh.shape["sector"], mesh.shape["term"]
    nx = terms // 2
    placed = (
        P("sector", None),
        P("term", "sector", None, None),
        P("term", "sector", None, None),
        P(),
        P(),
        P(),
        P(),
        P("term"),
    )
    return jax.shard_map(
        functools.partial(local, nx, sectors // nx),
        mesh=mesh,
        in_specs=placed,
        out_specs=P("sector", "term"),
        check_vma=False,
    )
```
